32 devices in a mesh: tok: 4 (over z), scol: 4 (over y, x), tcol: 2 (over core).
Axes of the slice: x: 2, y: 2, z: 4, core: 2. Of those that a mesh axis runs over, the one named last changes fastest.
Arguments:
- student: float32 [2048, 4096], P('tok', 'scol'), may hold values from -6 to 6
- teacher: float32 [2048, 4096], P('tok', 'tcol'), may hold values from -6 to 6
- teacher_norm: float32 [1], replicated, may hold values from 65536 to 262144
Outputs:
- student_grad: float32 [2048, 4096], P(('tok', 'tcol'), 'scol')
The draws below stay inside these ranges and needn't reach their ends.
All inputs are finite; a program needn't handle non-finite values.
Results may differ from the reference program's by a relative error of at most 0.000073.
Values sent between devices are 32-bit elements; how exact they have to be, the bound alone decides.
No kernel may reach another device: no remote copies, remote signals or barrier semaphores. Data moves between devices by JAX's collectives and lax.ppermute only.
A program may use at most 128 MiB of HBM per device.

```python
import math
import jax
import jax.numpy as jnp
from jax import lax

DS = 4096
DT = 4096
TOKENS = 2048


def shard_levels(rng, extent, cuts, low, largest):
    loudness = 1.0
    for position, parts in cuts:
        draws = jax.random.uniform(jax.random.fold_in(jax.random.fold_in(rng, 6), position), (parts,), jnp.float32, low / len(cuts), largest / len(cuts))
        loudness = loudness * jnp.repeat(jnp.exp(draws), extent[position] // parts).reshape((-1,) + (1,) * (len(extent) - 1 - position))
    return loudness


def scatter_about(own_key, extent, scale, bound, split=(), dtype=jnp.bfloat16):
    gain = shard_levels(own_key, extent, split, -0.22, 0.18) if split else 1.0
    drawn = jax.random.normal(own_key, extent, jnp.float32) * scale * gain
    return jnp.minimum(jnp.maximum(drawn, -bound), bound).astype(dtype)


def setup_inputs(seed: int = 0) -> dict:
    arg_keys = jax.random.split(jax.random.key(seed), 4)
    student = scatter_about(arg_keys[0], (TOKENS, DS), 1.0, 6.0, ((0, 4), (1, 4)), jnp.float32)
    teacher = scatter_about(arg_keys[1], (TOKENS, DT), 1.0, 6.0, ((0, 4), (1, 2)), jnp.float32)
    teacher_norm = jnp.clip(jnp.exp(jax.random.uniform(arg_keys[2], (1,), jnp.float32, math.log(65536.0), math.log(262144.0))), 65536.0, 262144.0)
    return {"student": student, "teacher": teacher, "teacher_norm": teacher_norm}


def reference(student, teacher, teacher_norm):
    highest = lax.Precision.HIGHEST
    cross = jnp.dot(student.T, teacher, precision=highest, preferred_element_type=jnp.float32)
    gram = jnp.dot(student.T, student, precision=highest, preferred_element_type=jnp.float32)
    hsic = jnp.sum(cross * cross)
    gram_sq = jnp.sum(gram * gram)
    student_norm = jnp.sqrt(gram_sq)
    factor = -2.0 * TOKENS * DS / (student_norm * teacher_norm[0])
    first = jnp.dot(teacher, cross.T, precision=highest, preferred_element_type=jnp.float32)
    second = jnp.dot(student, gram, precision=highest, preferred_element_type=jnp.float32)
    return factor * (first - hsic / gram_sq * second)
```

```python
import math

import jax
import jax.numpy as jnp
from jax import lax
from jax.experimental import pallas as pl
from jax.experimental.pallas import tpu as pltpu
from jax.sharding import PartitionSpec as P

VMEM = 40 * 1024 * 1024
PLANE = ("tok", "scol", "tcol")


def token_contract(left, right):
    return lax.dot_general(
        left,
        right,
        (((0,), (0,)), ((), ())),
        precision=lax.Precision.HIGHEST,
        preferred_element_type=jnp.float32,
    )


def feature_contract(left, right):
    return lax.dot_general(
        left,
        right,
        (((1,), (1,)), ((), ())),
        precision=lax.Precision.HIGHEST,
        preferred_element_type=jnp.float32,
    )


def feature_form(student, teacher, teacher_norm):
    col_index = lax.axis_index("tcol")
    tcol_count = lax.axis_size("tcol")
    tok_rows = student.shape[0]
    local_width = student.shape[1]
    features = local_width * lax.axis_size("scol")
    part_width = local_width // tcol_count
    own_slice = lax.dynamic_slice_in_dim(student, col_index * part_width, part_width, 1)
    partner = lax.all_gather(own_slice, "scol", axis=1, tiled=True)
    cov_block = token_contract(student, teacher)
    gram_block = token_contract(student, partner)
    cov_block, gram_block = lax.psum((cov_block, gram_block), "tok")
    local_stats = jnp.stack([jnp.sum(cov_block * cov_block), jnp.sum(gram_block * gram_block)])
    gathered = lax.all_gather(local_stats, ("scol", "tcol"), axis=0, tiled=True)
    totals = jnp.sum(gathered.reshape(-1, 2), axis=0)
    tokens_all = tok_rows * lax.axis_size("tok")
    factor = -2.0 * tokens_all * features / (jnp.sqrt(totals[1]) * teacher_norm[0])
    gram_ratio = totals[0] / totals[1]
    result = feature_contract(teacher, cov_block) - gram_ratio * feature_contract(
        partner, gram_block
    )
    return lax.psum_scatter(factor * result, "tcol", scatter_dimension=0, tiled=True)


PAIRS = [(0, 1), (1, 0), (2, 3), (3, 2)]
MIDDLE = [(1, 2), (2, 1)]
OUTWARD = [(1, 0), (2, 3)]
INWARD = [(0, 1), (3, 2)]
FAR = [(2, 0), (1, 3)]
CORES = [(0, 1), (1, 0)]


def chip_shift(shift):
    return [(c, c ^ shift) for c in range(4)]


def device_id(z, y, x, k):
    return ((z * 2 + y) * 2 + x) * 2 + k


def piece_shift(hi, lo):
    perm = []
    for z in range(4):
        for y in range(2):
            for x in range(2):
                for k in range(2):
                    if z in (0, 3):
                        perm.append((device_id(z, k, x ^ lo, y ^ hi), device_id(z, y, x, k)))
                    elif hi or lo:
                        perm.append((device_id(z, y ^ hi, x ^ lo, k), device_id(z, y, x, k)))
    return perm


def split(x):
    high = x.astype(jnp.bfloat16)
    return high, (x - high.astype(jnp.float32)).astype(jnp.bfloat16)


def dot(left, right, dims):
    return lax.dot_general(left, right, (dims, ((), ())), preferred_element_type=jnp.float32)


def dot_split(left, right, dims):
    (lh, ll), (rh, rl) = left, right
    return dot(lh, rh, dims) + dot(lh, rl, dims) + dot(ll, rh, dims)


ROWS = ((1,), (1,))
COLS = ((1,), (0,))
FLAGS = pl.BlockSpec(memory_space=pltpu.SMEM)


def call(kernel, flags, args, outs, flops=0):
    moved = sum(a.size * 4 for a in args) + sum(math.prod(o) * 4 for o in outs)
    whole = pl.BlockSpec(memory_space=pltpu.VMEM)
    return pl.pallas_call(
        kernel,
        out_shape=[jax.ShapeDtypeStruct(o, jnp.float32) for o in outs],
        in_specs=[FLAGS] + [whole] * len(args),
        out_specs=[whole] * len(outs),
        compiler_params=pltpu.CompilerParams(vmem_limit_bytes=VMEM),
        cost_estimate=pl.CostEstimate(flops=flops, bytes_accessed=moved, transcendentals=0),
    )(flags, *args)


def gram_parts(flags, own, pairs):
    half = own.shape[0]

    def kernel(flags_ref, own_ref, *refs):
        left = split(own_ref[...])
        n = len(pairs)
        for g in range(n):
            for side in range(2):
                refs[2 * n + side][:, g * half : (g + 1) * half] = dot_split(
                    left, split(refs[2 * g + side][...]), ROWS
                )

    flat = [part for pair in pairs for part in pair]
    flops = 6 * half * own.shape[1] * half * len(flat)
    return call(kernel, flags, [own] + flat, [(half, half * len(pairs))] * 2, flops)


def teacher_parts(flags, teacher, other):
    rows, width = teacher.shape
    half, n = rows // 2, other.shape[0]
    step = width // 4

    def kernel(flags_ref, teacher_ref, other_ref, kept_ref, away_ref):
        k = flags_ref[0]
        right = split(other_ref[...])
        for out_ref, which in ((away_ref, 1 - k), (kept_ref, k)):
            mine = teacher_ref[pl.ds(pl.multiple_of(which * half, half), half), :]
            part = dot_split(split(mine), right, ROWS)

            @pl.when(pl.program_id(0) == 0)
            def _():
                out_ref[...] = part

            @pl.when(pl.program_id(0) > 0)
            def _():
                out_ref[...] += part

    return pl.pallas_call(
        kernel,
        grid=(4,),
        out_shape=[jax.ShapeDtypeStruct((half, n), jnp.float32)] * 2,
        in_specs=[
            FLAGS,
            pl.BlockSpec((rows, step), lambda i: (0, i)),
            pl.BlockSpec((n, step), lambda i: (0, i)),
        ],
        out_specs=[pl.BlockSpec((half, n), lambda i: (0, 0))] * 2,
        compiler_params=pltpu.CompilerParams(vmem_limit_bytes=VMEM),
        cost_estimate=pl.CostEstimate(
            flops=6 * rows * width * n, bytes_accessed=4 * (rows * width + n * width + rows * n), transcendentals=0
        ),
    )(flags, teacher, other)


def ordered(flags_ref, pieces):
    lo, hi = flags_ref[2] == 1, flags_ref[3] == 1
    g00, g01, g10, g11 = pieces
    a0, a1 = jnp.where(lo, g01, g00), jnp.where(lo, g00, g01)
    b0, b1 = jnp.where(lo, g11, g10), jnp.where(lo, g10, g11)
    low, high = jnp.concatenate([a0, a1], 1), jnp.concatenate([b0, b1], 1)
    return jnp.where(hi, high, low), jnp.where(hi, low, high)


def gathered(flags, pieces, returned=None):
    half = pieces[0].shape[0]
    width = half // 2
    n = pieces[0].shape[1] // width
    args = list(pieces) + ([] if returned is None else [returned])

    def kernel(flags_ref, *refs):
        left_ref, right_ref = refs[-2:]
        edge = flags_ref[1] == 1
        for g in range(n):
            at = slice(g * width, (g + 1) * width)
            parts = [ref[:, at] for ref in refs[:4]]
            if returned is not None:
                parts[0] = jnp.where(edge, refs[4][:, at], parts[0])
            left, right = ordered(flags_ref, parts)
            if returned is not None:
                left, right = jnp.where(edge, left.T, left), jnp.where(edge, right.T, right)
            left_ref[:, g * half : (g + 1) * half] = left
            right_ref[:, g * half : (g + 1) * half] = right

    return call(kernel, flags, args, [(half, half * n)] * 2)


def first_products(flags, kt, ks, s):
    half, width = s[0].shape
    chunk = width // 4
    n_s = len(s)
    flat_kt = [part for pair in kt for part in pair]
    flat_ks = [part for quad in ks for part in quad]

    def kernel(flags_ref, *refs):
        kt_refs = refs[: len(flat_kt)]
        ks_refs = refs[len(flat_kt) : len(flat_kt) + len(flat_ks)]
        s_refs = refs[len(flat_kt) + len(flat_ks) :][:n_s]
        out_ref, sum_ref, high, low = refs[-4:]

        @pl.when(pl.program_id(0) == 0)
        def _():
            edge = flags_ref[1] == 1
            (kt_own, kt_rest) = kt_refs[:2], kt_refs[2:]
            hsic = gram = jnp.zeros((1, 1), jnp.float32)
            for side in range(2):
                own_s, a_s = (q[2 * side][...] + q[2 * side + 1][...] for q in (ks_refs[0:4], ks_refs[4:8]))
                bc_s = ks_refs[8 + 2 * side][...] + ks_refs[9 + 2 * side][...]
                rest = kt_rest[side][...]
                two = rest[:, half:]
                zero = jnp.zeros_like(two)
                top = [kt_own[side][...], rest[:, :half], jnp.where(edge, two, zero), jnp.where(edge, zero, two)]
                bottom = [own_s, a_s, bc_s[:, :half], bc_s[:, half:]]
                for g in range(4):
                    at = slice((2 * g + side) * half, (2 * g + side + 1) * half)
                    high[:half, at], low[:half, at] = split(top[g])
                    high[half:, at], low[half:, at] = split(bottom[g])
                    hsic = hsic + jnp.sum(top[g] * bottom[g], keepdims=True)
                    gram = gram + jnp.sum(bottom[g] * bottom[g], keepdims=True)
            row = lax.broadcasted_iota(jnp.int32, sum_ref.shape, 0)
            sum_ref[...] = jnp.where(row < 4, hsic, gram)

        total = None
        for i in range(n_s):
            at = slice(i * half, (i + 1) * half)
            part = dot_split((high[:, at], low[:, at]), split(s_refs[i][...]), COLS)
            total = part if total is None else total + part
        out_ref[...] = total

    whole = pl.BlockSpec(memory_space=pltpu.VMEM)
    return pl.pallas_call(
        kernel,
        grid=(4,),
        out_shape=[
            jax.ShapeDtypeStruct((2 * half, width), jnp.float32),
            jax.ShapeDtypeStruct((8, 128), jnp.float32),
        ],
        in_specs=[FLAGS]
        + [whole] * (len(flat_kt) + len(flat_ks))
        + [pl.BlockSpec((half, chunk), lambda i: (0, i))] * n_s,
        out_specs=[
            pl.BlockSpec((2 * half, chunk), lambda i: (0, i)),
            pl.BlockSpec((8, 128), lambda i: (0, 0)),
        ],
        scratch_shapes=[pltpu.VMEM((2 * half, half * n_s), jnp.bfloat16)] * 2,
        compiler_params=pltpu.CompilerParams(vmem_limit_bytes=VMEM),
        cost_estimate=pl.CostEstimate(
            flops=6 * 2 * half * half * n_s * width, bytes_accessed=16 * half * width, transcendentals=0
        ),
    )(flags, *flat_kt, *flat_ks, *s)


def last_sums(flags, pieces, ks, sums):
    half = pieces[0].shape[0]

    def kernel(flags_ref, p0, p1, p2, p3, l1, l2, r1, r2, sum_ref, left_ref, right_ref, out_ref):
        edge = flags_ref[1] == 1
        left, right = ordered(flags_ref, [p[...] for p in (p0, p1, p2, p3)])
        left_ref[...], right_ref[...] = left, right
        ks_left, ks_right = l1[...] + l2[...], r1[...] + r2[...]
        ks_left = jnp.where(edge, ks_left[:, half:], ks_left[:, :half])
        ks_right = jnp.where(edge, ks_right[:, half:], ks_right[:, :half])
        hsic = jnp.sum(left * ks_left + right * ks_right, keepdims=True)
        row = lax.broadcasted_iota(jnp.int32, out_ref.shape, 0)
        out_ref[...] = sum_ref[...] + jnp.where(row < 4, hsic, 0.0)

    return call(kernel, flags, [*pieces, *ks, sums], [(half, half)] * 2 + [(8, 128)])


def finish(flags, kt, s_b, s_c, products, sums, norm, scale):
    half, width = s_b[0].shape

    def kernel(flags_ref, l_ref, r_ref, bl, br, cl, cr, prod_ref, sum_ref, norm_ref, out_ref):
        hsic, gram = sum_ref[0:1, 0:1], sum_ref[4:5, 0:1]
        factor = scale / (jnp.sqrt(gram) * norm_ref[0:1, 0:1])
        ratio = hsic / gram
        left, right = split(l_ref[...]), split(r_ref[...])

        def put(first, second):
            total = prod_ref[:half, :] - ratio * prod_ref[half:, :]
            total = total + dot_split(left, split(first[...]), COLS)
            total = total + dot_split(right, split(second[...]), COLS)
            out_ref[...] = factor * total

        @pl.when(flags_ref[1] == 1)
        def _():
            put(cl, cr)

        @pl.when(flags_ref[1] == 0)
        def _():
            put(bl, br)

    return call(
        kernel, flags, [*kt, *s_b, *s_c, products, sums, norm], [(half, width)], 12 * half * half * width
    )[0]


def token_form(student, teacher, teacher_norm):
    z = lax.axis_index("tok")
    c = lax.axis_index("scol")
    k = lax.axis_index("tcol")
    rows = student.shape[0]
    half = rows // 2
    quarter = rows // 4
    tokens_all = rows * lax.axis_size("tok")
    features = student.shape[1] * lax.axis_size("scol")
    edge = jnp.logical_or(z == 0, z == 3)
    flags = jnp.stack([k, edge.astype(jnp.int32), c % 2, (c // 2 != k).astype(jnp.int32)])
    step = lax.optimization_barrier

    def send(x, perm):
        return lax.ppermute(x, "tok", perm)

    def both_halves(mine):
        return mine, lax.ppermute(mine, "tcol", CORES)

    def chip_sum(parts):
        left, right = parts
        left = left + lax.ppermute(left, "scol", chip_shift(1))
        right = right + lax.ppermute(right, "scol", chip_shift(2))
        return [
            left,
            lax.ppermute(left, "scol", chip_shift(2)),
            right,
            lax.ppermute(right, "scol", chip_shift(1)),
        ]

    def teacher_piece(other):
        kept, away = teacher_parts(flags, teacher, other)
        return kept + lax.ppermute(away, "tcol", CORES)

    def same_plane(piece):
        return [piece] + [lax.ppermute(piece, "scol", chip_shift(s)) for s in (1, 2, 3)]

    s_half = lax.dynamic_slice_in_dim(student, k * half, half, 0)
    near, mid = send(s_half, PAIRS), send(s_half, MIDDLE)
    t_quarter = lax.dynamic_slice_in_dim(teacher, c * quarter, quarter, 0)
    s_own = (s_half, lax.dynamic_slice_in_dim(student, (1 - k) * half, half, 0))
    part_own = gram_parts(flags, s_half, [s_own])
    ks_own = chip_sum(part_own)
    piece_own = teacher_piece(t_quarter)
    near, mid, ks_own, piece_own, t_quarter = step((near, mid, ks_own, piece_own, t_quarter))

    far_edge, far_mid = send(mid, OUTWARD), send(near, MIDDLE)
    t_in = send(t_quarter, INWARD)
    s_a = both_halves(near)
    ks_a = chip_sum(gram_parts(flags, s_half, [s_a]))
    kt_own = gathered(flags, same_plane(piece_own))
    far_edge, far_mid, t_in, mid, t_quarter, s_a, kt_own, ks_a = step(
        (far_edge, far_mid, t_in, mid, t_quarter, s_a, kt_own, ks_a)
    )

    last_edge, t_cross = send(far_mid, OUTWARD), send(t_in, MIDDLE)
    s_b = both_halves(jnp.where(edge, far_edge, mid))
    piece_in = teacher_piece(t_in)
    back_in = send(piece_in, OUTWARD)
    last_edge, t_cross, far_mid, t_quarter, s_b, piece_in, back_in = step(
        (last_edge, t_cross, far_mid, t_quarter, s_b, piece_in, back_in)
    )

    t_edge, t_mid = send(t_cross, OUTWARD), send(t_quarter, MIDDLE)
    s_c = both_halves(jnp.where(edge, last_edge, far_mid))
    piece_cross = teacher_piece(t_cross)
    back_cross = send(piece_cross, FAR)
    ks_bc = chip_sum(gram_parts(flags, s_half, [s_b, s_c]))
    piece = jnp.concatenate(
        [jnp.where(edge, back_in, piece_in), jnp.where(edge, back_cross, piece_cross)], 1
    )
    moved = [lax.ppermute(piece, PLANE, piece_shift(hi, lo)) for hi, lo in ((0, 1), (1, 0), (1, 1))]
    kt_rest = gathered(flags, [piece] + moved, lax.ppermute(piece, PLANE, piece_shift(0, 0)))
    t_last = jnp.where(edge, t_edge, t_mid)

    pieces = same_plane(teacher_piece(t_last))
    products, sums = first_products(
        flags, [kt_own, kt_rest], [ks_own, ks_a, ks_bc], [*s_own, *s_a, *s_b, *s_c]
    )
    left, right, sums = last_sums(flags, pieces, ks_bc, sums)
    sums = sums + lax.ppermute(sums, "tcol", CORES)
    sums = sums + lax.ppermute(sums, "tok", PAIRS)
    sums = sums + lax.ppermute(sums, "tok", [(0, 2), (2, 0), (1, 3), (3, 1)])
    return finish(
        flags, (left, right), s_b, s_c, products, sums, teacher_norm.reshape(1, 1), -2.0 * tokens_all * features
    )


def solution(mesh):
    sizes = (mesh.shape["tok"], mesh.shape["scol"], mesh.shape["tcol"])

    def body(student, teacher, teacher_norm):
        tokens_all = student.shape[0] * sizes[0]
        features = student.shape[1] * sizes[1]
        if sizes == (4, 4, 2) and tokens_all <= features:
            return token_form(student, teacher, teacher_norm)
        return feature_form(student, teacher, teacher_norm)

    return jax.shard_map(
        body,
        mesh=mesh,
        in_specs=(P("tok", "scol"), P("tok", "tcol"), P()),
        out_specs=P(("tok", "tcol"), "scol"),
        check_vma=False,
    )
```

```python
import math

import jax
import jax.numpy as jnp
from jax import lax
from jax.experimental import pallas as pl
from jax.experimental.pallas import tpu as pltpu
from jax.sharding import PartitionSpec as P

LIGHT = pl.CostEstimate(flops=0, bytes_accessed=0, transcendentals=0)
PLANE = ("tok", "scol", "tcol")


def token_contract(left, right):
    return lax.dot_general(
        left,
        right,
        (((0,), (0,)), ((), ())),
        precision=lax.Precision.HIGHEST,
        preferred_element_type=jnp.float32,
    )


def feature_contract(left, right):
    return lax.dot_general(
        left,
        right,
        (((1,), (1,)), ((), ())),
        precision=lax.Precision.HIGHEST,
        preferred_element_type=jnp.float32,
    )


def feature_form(student, teacher, teacher_norm):
    col_index = lax.axis_index("tcol")
    tcol_count = lax.axis_size("tcol")
    tok_rows = student.shape[0]
    local_width = student.shape[1]
    features = local_width * lax.axis_size("scol")
    part_width = local_width // tcol_count
    own_slice = lax.dynamic_slice_in_dim(student, col_index * part_width, part_width, 1)
    partner = lax.all_gather(own_slice, "scol", axis=1, tiled=True)
    cov_block = token_contract(student, teacher)
    gram_block = token_contract(student, partner)
    cov_block, gram_block = lax.psum((cov_block, gram_block), "tok")
    local_stats = jnp.stack([jnp.sum(cov_block * cov_block), jnp.sum(gram_block * gram_block)])
    gathered = lax.all_gather(local_stats, ("scol", "tcol"), axis=0, tiled=True)
    totals = jnp.sum(gathered.reshape(-1, 2), axis=0)
    tokens_all = tok_rows * lax.axis_size("tok")
    factor = -2.0 * tokens_all * features / (jnp.sqrt(totals[1]) * teacher_norm[0])
    gram_ratio = totals[0] / totals[1]
    result = feature_contract(teacher, cov_block) - gram_ratio * feature_contract(
        partner, gram_block
    )
    return lax.psum_scatter(factor * result, "tcol", scatter_dimension=0, tiled=True)


PAIRS = [(0, 1), (1, 0), (2, 3), (3, 2)]
MIDDLE = [(1, 2), (2, 1)]
OUTWARD = [(1, 0), (2, 3)]
INWARD = [(0, 1), (3, 2)]
FAR = [(2, 0), (1, 3)]
CORES = [(0, 1), (1, 0)]


def chip_shift(shift):
    return [(c, c ^ shift) for c in range(4)]


def device_id(z, y, x, k):
    return ((z * 2 + y) * 2 + x) * 2 + k


def piece_shift(hi, lo):
    perm = []
    for z in range(4):
        for y in range(2):
            for x in range(2):
                for k in range(2):
                    if z in (0, 3):
                        perm.append((device_id(z, k, x ^ lo, y ^ hi), device_id(z, y, x, k)))
                    elif hi or lo:
                        perm.append((device_id(z, y ^ hi, x ^ lo, k), device_id(z, y, x, k)))
    return perm


def split(x):
    high = x.astype(jnp.bfloat16)
    return high, (x - high.astype(jnp.float32)).astype(jnp.bfloat16)


def dot(left, right, dims):
    return lax.dot_general(left, right, (dims, ((), ())), preferred_element_type=jnp.float32)


def dot_split(left, right, dims):
    (lh, ll), (rh, rl) = left, right
    return dot(lh, rh, dims) + dot(lh, rl, dims) + dot(ll, rh, dims)


ROWS = ((1,), (1,))
COLS = ((1,), (0,))
FLAGS = pl.BlockSpec(memory_space=pltpu.SMEM)


def room(args, outs, scratch=0):
    total = sum(math.prod(a.shape) * a.dtype.itemsize for a in (*args, *outs)) + scratch
    return pltpu.CompilerParams(vmem_limit_bytes=total + total // 4 + (6 << 20))


def call(kernel, flags, args, outs):
    outs = [jax.ShapeDtypeStruct(o, jnp.float32) for o in outs]
    whole = pl.BlockSpec(memory_space=pltpu.VMEM)
    return pl.pallas_call(
        kernel,
        out_shape=outs,
        in_specs=[FLAGS] + [whole] * len(args),
        out_specs=[whole] * len(outs),
        compiler_params=room(args, outs),
        cost_estimate=LIGHT,
    )(flags, *args)


def gram_part(flags, own, pair):
    half = own.shape[0]

    def kernel(flags_ref, own_ref, first_ref, second_ref, *outs):
        left = split(own_ref[...])
        for ref, out_ref in zip((first_ref, second_ref), outs):
            out_ref[...] = dot_split(left, split(ref[...]), ROWS)

    return call(kernel, flags, [own, *pair], [(half, half)] * 2)


def summed(refs, side):
    return refs[2 * side][...] + refs[2 * side + 1][...]


def teacher_parts(flags, teacher, others, keep_split=False):
    rows, width = teacher[0].shape
    half = rows // 2
    flat = [array for other in others for array in (other if isinstance(other, tuple) else (other,))]
    n = sum((other[0] if isinstance(other, tuple) else other).shape[0] for other in others)
    step = width // 4

    def kernel(flags_ref, *refs):
        teacher_refs, other_refs = refs[: len(teacher)], refs[len(teacher) :][: len(flat)]
        outs = refs[len(teacher) + len(flat) :]
        edge = flags_ref[1] == 1
        for i in range(4):
            at = slice(i * step, (i + 1) * step)
            taken = iter(other_refs)
            right = []
            for other in others:
                value = next(taken)[:, at]
                if isinstance(other, tuple):
                    value = jnp.where(edge, value, next(taken)[:, at])
                right.append(value)
            high, low = split(right[0] if len(right) == 1 else jnp.concatenate(right, 0))
            both = jnp.concatenate([high, low], 0)
            for out_ref, which in ((outs[1], 1 - flags_ref[0]), (outs[0], flags_ref[0])):
                mine = pl.ds(pl.multiple_of(which * half, half), half)
                if len(teacher) == 1:
                    th, tl = split(teacher_refs[0][mine, at])
                    if keep_split:
                        outs[2][mine, at], outs[3][mine, at] = th, tl
                else:
                    th, tl = (ref[mine, at] for ref in teacher_refs)
                part = dot(th, both, ROWS)
                part = part[:, :n] + part[:, n:] + dot(tl, high, ROWS)
                if i == 0:
                    out_ref[...] = part
                else:
                    out_ref[...] += part

    whole = pl.BlockSpec(memory_space=pltpu.VMEM)
    outs = [jax.ShapeDtypeStruct((half, n), jnp.float32)] * 2
    if keep_split:
        outs += [jax.ShapeDtypeStruct((rows, width), jnp.bfloat16)] * 2
    return pl.pallas_call(
        kernel,
        out_shape=outs,
        in_specs=[FLAGS] + [whole] * (len(teacher) + len(flat)),
        out_specs=[whole] * len(outs),
        compiler_params=room([*teacher, *flat], outs),
        cost_estimate=LIGHT,
    )(flags, *teacher, *flat)


def ordered(flags_ref, pieces):
    lo, hi = flags_ref[2] == 1, flags_ref[3] == 1
    g00, g01, g10, g11 = pieces
    a0, a1 = jnp.where(lo, g01, g00), jnp.where(lo, g00, g01)
    b0, b1 = jnp.where(lo, g11, g10), jnp.where(lo, g10, g11)
    low, high = jnp.concatenate([a0, a1], 1), jnp.concatenate([b0, b1], 1)
    return jnp.where(hi, high, low), jnp.where(hi, low, high)


def pick(flags_ref, first, second):
    return jnp.where(flags_ref[1] == 1, first, second)


def spread(sum_ref, hsic, gram):
    row = lax.broadcasted_iota(jnp.int32, sum_ref.shape, 0)
    return jnp.where(row < 4, hsic, gram)


def products_call(kernel, flags, args, out, scratch):
    outs = [jax.ShapeDtypeStruct(shape, jnp.float32) for shape in (out, (8, 128))]
    whole = pl.BlockSpec(memory_space=pltpu.VMEM)
    return pl.pallas_call(
        kernel,
        out_shape=outs,
        in_specs=[FLAGS] + [whole] * len(args),
        out_specs=[whole] * 2,
        scratch_shapes=[pltpu.VMEM(scratch, jnp.bfloat16)] * 2,
        compiler_params=room(args, outs, 4 * math.prod(scratch)),
        cost_estimate=LIGHT,
    )(flags, *args)


def first_products(flags, ks, s):
    half, width = s[0].shape
    chunk = width // 4

    def kernel(flags_ref, *refs):
        ks_refs, s_refs = refs[:12], refs[12:18]
        out_ref, sum_ref, high, low = refs[18:]
        gram = jnp.zeros((1, 1), jnp.float32)
        for g in range(3):
            for side in range(2):
                at = slice((2 * g + side) * half, (2 * g + side + 1) * half)
                bottom = summed(ks_refs[4 * g : 4 * g + 4], side)
                high[:, at], low[:, at] = split(bottom)
                gram = gram + jnp.sum(bottom * bottom, keepdims=True)
        sum_ref[...] = spread(sum_ref, 0.0, gram)
        for j in range(4):
            cols = slice(j * chunk, (j + 1) * chunk)
            total = 0.0
            for i in range(6):
                at = slice(i * half, (i + 1) * half)
                total = total + dot_split((high[:, at], low[:, at]), split(s_refs[i][:, cols]), COLS)
            out_ref[:, cols] = total

    args = [part for quad in ks for part in quad] + list(s)
    return products_call(kernel, flags, args, [half, width], [half, 6 * half])


def second_products(flags, own, first, ks, s, products, sums):
    half, width = s[0].shape
    chunk = width // 4

    def kernel(flags_ref, *refs):
        own_refs, first_refs, refs = refs[:4], refs[4:9], refs[9:]
        ks_refs, s_refs, (prod_ref, before_ref) = refs[:16], refs[16:24], refs[24:26]
        edge = flags_ref[1] == 1
        tops = [ordered(flags_ref, [ref[...] for ref in own_refs])]
        for g in range(2):
            at = slice(g * half // 2, (g + 1) * half // 2)
            pieces = [ref[:, at] for ref in first_refs]
            left, right = ordered(flags_ref, [jnp.where(edge, pieces[4], pieces[0]), *pieces[1:4]])
            tops.append((jnp.where(edge, left.T, left), jnp.where(edge, right.T, right)))
        out_ref, sum_ref, high, low = refs[26:]
        hsic = gram = jnp.zeros((1, 1), jnp.float32)
        for side in range(2):
            own, a, b, c = (summed(ks_refs[4 * g : 4 * g + 4], side) for g in range(4))
            for g, bottom in enumerate((own, a, pick(flags_ref, b, c))):
                at = slice((2 * g + side) * half, (2 * g + side + 1) * half)
                top = tops[g][side]
                high[:, at], low[:, at] = split(top)
                hsic = hsic + jnp.sum(top * bottom, keepdims=True)
            at = slice((6 + side) * half, (7 + side) * half)
            high[:, at], low[:, at] = split(c)
            gram = gram + jnp.sum(c * c, keepdims=True)
        sum_ref[...] = before_ref[...] + spread(sum_ref, hsic, gram)
        for j in range(4):
            cols = slice(j * chunk, (j + 1) * chunk)
            upper, lower = 0.0, prod_ref[:, cols]
            for side in range(2):
                own, a, b, c = (s_refs[2 * g + side][:, cols] for g in range(4))
                for g, part in enumerate((own, a, pick(flags_ref, b, c), c)):
                    at = slice((2 * g + side) * half, (2 * g + side + 1) * half)
                    part = dot_split((high[:, at], low[:, at]), split(part), COLS)
                    if g < 3:
                        upper = upper + part
                    else:
                        lower = lower + part
            out_ref[:half, cols] = upper
            out_ref[half:, cols] = lower

    args = [*own, *first, *[part for quad in ks for part in quad], *s, products, sums]
    return products_call(kernel, flags, args, [2 * half, width], [half, 8 * half])


def last_sums(flags, pieces, ks_b, ks_c, sums):
    half = pieces[0].shape[0]

    def kernel(flags_ref, p0, p1, p2, p3, *refs):
        b_refs, c_refs, (sum_ref, left_ref, right_ref, out_ref) = refs[:4], refs[4:8], refs[8:]
        tops = ordered(flags_ref, [p[...] for p in (p0, p1, p2, p3)])
        left_ref[...], right_ref[...] = tops
        hsic = jnp.zeros((1, 1), jnp.float32)
        for side in range(2):
            bottom = pick(flags_ref, summed(c_refs, side), summed(b_refs, side))
            hsic = hsic + jnp.sum(tops[side] * bottom, keepdims=True)
        out_ref[...] = sum_ref[...] + spread(out_ref, hsic, 0.0)

    return call(kernel, flags, [*pieces, *ks_b, *ks_c, sums], [(half, half)] * 2 + [(8, 128)])


def last_products(flags, kt, s, products):
    half, width = s[0].shape
    chunk = width // 4

    def kernel(flags_ref, l_ref, r_ref, bl, br, cl, cr, prod_ref, out_ref):
        left, right = split(l_ref[...]), split(r_ref[...])
        for j in range(4):
            cols = slice(j * chunk, (j + 1) * chunk)
            total = prod_ref[:half, cols]
            total = total + dot_split(left, split(pick(flags_ref, cl[:, cols], bl[:, cols])), COLS)
            total = total + dot_split(right, split(pick(flags_ref, cr[:, cols], br[:, cols])), COLS)
            out_ref[:, cols] = total

    return call(kernel, flags, [*kt, *s, products], [(half, width)])[0]


def finish(flags, upper, products, sums, norm, scale):
    half, width = upper.shape

    def kernel(flags_ref, up_ref, prod_ref, norm_ref, *refs):
        total = sum(ref[...] for ref in refs[:-1])
        hsic, gram = total[0:1, 0:1], total[4:5, 0:1]
        factor = scale / (jnp.sqrt(gram) * norm_ref[0:1, 0:1])
        refs[-1][...] = factor * (up_ref[...] - (hsic / gram) * prod_ref[half:, :])

    return call(kernel, flags, [upper, products, norm, *sums], [(half, width)])[0]


def token_form(student, teacher, teacher_norm):
    z = lax.axis_index("tok")
    c = lax.axis_index("scol")
    k = lax.axis_index("tcol")
    rows = student.shape[0]
    half = rows // 2
    quarter = rows // 4
    tokens_all = rows * lax.axis_size("tok")
    features = student.shape[1] * lax.axis_size("scol")
    edge = jnp.logical_or(z == 0, z == 3)
    flags = jnp.stack([k, edge.astype(jnp.int32), c % 2, (c // 2 != k).astype(jnp.int32)])
    step = lax.optimization_barrier

    def send(x, perm):
        return lax.ppermute(x, "tok", perm)

    def both_halves(mine):
        return mine, lax.ppermute(mine, "tcol", CORES)

    def sum_x_y(left, right):
        left = left + lax.ppermute(left, "scol", chip_shift(1))
        right = right + lax.ppermute(right, "scol", chip_shift(2))
        return left, right

    def terms_y_x(left, right):
        return [
            left,
            lax.ppermute(left, "scol", chip_shift(2)),
            right,
            lax.ppermute(right, "scol", chip_shift(1)),
        ]

    def chip_sum(parts):
        return terms_y_x(*sum_x_y(*parts))

    def swap_rows(kept, away):
        return kept + lax.ppermute(away, "tcol", CORES)

    def same_plane(piece):
        return [piece] + [lax.ppermute(piece, "scol", chip_shift(s)) for s in (1, 2, 3)]

    def mixed(piece):
        return [piece] + [
            lax.ppermute(piece, PLANE, piece_shift(hi, lo)) for hi, lo in ((0, 1), (1, 0), (1, 1), (0, 0))
        ]

    s_half = lax.dynamic_slice_in_dim(student, k * half, half, 0)
    near, mid = send(s_half, PAIRS), send(s_half, MIDDLE)
    s_own = (s_half, lax.dynamic_slice_in_dim(student, (1 - k) * half, half, 0))
    ks_own = chip_sum(gram_part(flags, s_half, s_own))
    t_quarter = lax.dynamic_slice_in_dim(teacher, c * quarter, quarter, 0)
    kept, away, *t_split = teacher_parts(flags, [teacher], [t_quarter], True)
    own = swap_rows(kept, away)
    near, mid, t_quarter, ks_own, own, t_split = step((near, mid, t_quarter, ks_own, own, t_split))

    far_edge, far_mid = send(mid, OUTWARD), send(near, MIDDLE)
    t_in = send(t_quarter, INWARD)
    pieces_own = same_plane(own)
    s_a = both_halves(near)
    ks_a = chip_sum(gram_part(flags, s_half, s_a))
    far_edge, far_mid, t_in, mid, t_quarter, s_a, ks_a, pieces_own = step(
        (far_edge, far_mid, t_in, mid, t_quarter, s_a, ks_a, pieces_own)
    )

    last_edge, t_cross = send(far_mid, OUTWARD), send(t_in, MIDDLE)
    s_b = both_halves(jnp.where(edge, far_edge, mid))
    first = swap_rows(*teacher_parts(flags, t_split, [t_in]))
    back_in = send(first, OUTWARD)
    ks_b = chip_sum(gram_part(flags, s_half, s_b))
    last_edge, t_cross, far_mid, t_quarter, s_b, first, ks_b = step(
        (last_edge, t_cross, far_mid, t_quarter, s_b, first, ks_b)
    )

    part = quarter // 2
    edge_1, mid_1 = send(t_cross[:part], OUTWARD), send(t_quarter[:part], MIDDLE)
    cross = swap_rows(*teacher_parts(flags, t_split, [t_cross]))
    back_cross = send(cross, FAR)
    s_c = both_halves(jnp.where(edge, last_edge, far_mid))
    part_c = sum_x_y(*gram_part(flags, s_half, s_c))
    products, sums = first_products(flags, [ks_own, ks_a, ks_b], [*s_own, *s_a, *s_b])
    edge_1, mid_1, t_cross, t_quarter, back_in, part_c, cross, products, sums = step(
        (edge_1, mid_1, t_cross, t_quarter, back_in, part_c, cross, products, sums)
    )
    edge_2, mid_2 = send(t_cross[part:], OUTWARD), send(t_quarter[part:], MIDDLE)
    ks_c = terms_y_x(*part_c)
    pieces_first = mixed(jnp.concatenate([jnp.where(edge, back_in, first), jnp.where(edge, back_cross, cross)], 1))
    edge_2, mid_2, pieces_first = step((edge_2, mid_2, pieces_first))

    pieces = same_plane(swap_rows(*teacher_parts(flags, t_split, [(edge_1, mid_1), (edge_2, mid_2)])))
    s_all, ks_all = [*s_own, *s_a, *s_b, *s_c], [ks_own, ks_a, ks_b, ks_c]
    products, sums = second_products(flags, pieces_own, pieces_first, ks_all, s_all, products, sums)
    left, right, sums = last_sums(flags, pieces, ks_b, ks_c, sums)
    sums = sums + lax.ppermute(sums, "tcol", CORES)
    planes = [sums] + [lax.ppermute(sums, "tok", [(i, (i + s) % 4) for i in range(4)]) for s in (1, 2, 3)]
    upper = last_products(flags, (left, right), [*s_b, *s_c], products)
    scale = -2.0 * tokens_all * features
    return finish(flags, upper, products, planes, teacher_norm.reshape(1, 1), scale)


def solution(mesh):
    sizes = (mesh.shape["tok"], mesh.shape["scol"], mesh.shape["tcol"])

    def body(student, teacher, teacher_norm):
        tokens_all = student.shape[0] * sizes[0]
        features = student.shape[1] * sizes[1]
        if sizes == (4, 4, 2) and tokens_all <= features:
            return token_form(student, teacher, teacher_norm)
        return feature_form(student, teacher, teacher_norm)

    return jax.shard_map(
        body,
        mesh=mesh,
        in_specs=(P("tok", "scol"), P("tok", "tcol"), P()),
        out_specs=P(("tok", "tcol"), "scol"),
        check_vma=False,
    )
```

```python
import math

import jax
import jax.numpy as jnp
from jax import lax
from jax.experimental import pallas as pl
from jax.experimental.pallas import tpu as pltpu
from jax.sharding import PartitionSpec as P

LIGHT = pl.CostEstimate(flops=0, bytes_accessed=0, transcendentals=0)
PLANE = ("tok", "scol", "tcol")


def token_contract(left, right):
    return lax.dot_general(
        left,
        right,
        (((0,), (0,)), ((), ())),
        precision=lax.Precision.HIGHEST,
        preferred_element_type=jnp.float32,
    )


def feature_contract(left, right):
    return lax.dot_general(
        left,
        right,
        (((1,), (1,)), ((), ())),
        precision=lax.Precision.HIGHEST,
        preferred_element_type=jnp.float32,
    )


def feature_form(student, teacher, teacher_norm):
    col_index = lax.axis_index("tcol")
    tcol_count = lax.axis_size("tcol")
    tok_rows = student.shape[0]
    local_width = student.shape[1]
    features = local_width * lax.axis_size("scol")
    part_width = local_width // tcol_count
    own_slice = lax.dynamic_slice_in_dim(student, col_index * part_width, part_width, 1)
    partner = lax.all_gather(own_slice, "scol", axis=1, tiled=True)
    cov_block = token_contract(student, teacher)
    gram_block = token_contract(student, partner)
    cov_block, gram_block = lax.psum((cov_block, gram_block), "tok")
    local_stats = jnp.stack([jnp.sum(cov_block * cov_block), jnp.sum(gram_block * gram_block)])
    gathered = lax.all_gather(local_stats, ("scol", "tcol"), axis=0, tiled=True)
    totals = jnp.sum(gathered.reshape(-1, 2), axis=0)
    tokens_all = tok_rows * lax.axis_size("tok")
    factor = -2.0 * tokens_all * features / (jnp.sqrt(totals[1]) * teacher_norm[0])
    gram_ratio = totals[0] / totals[1]
    result = feature_contract(teacher, cov_block) - gram_ratio * feature_contract(
        partner, gram_block
    )
    return lax.psum_scatter(factor * result, "tcol", scatter_dimension=0, tiled=True)


PAIRS = [(0, 1), (1, 0), (2, 3), (3, 2)]
MIDDLE = [(1, 2), (2, 1)]
OUTWARD = [(1, 0), (2, 3)]
INWARD = [(0, 1), (3, 2)]
FAR = [(2, 0), (1, 3)]
CORES = [(0, 1), (1, 0)]


def chip_shift(shift):
    return [(c, c ^ shift) for c in range(4)]


def device_id(z, y, x, k):
    return ((z * 2 + y) * 2 + x) * 2 + k


def piece_shift(hi, lo):
    perm = []
    for z in range(4):
        for y in range(2):
            for x in range(2):
                for k in range(2):
                    if z in (0, 3):
                        perm.append((device_id(z, k, x ^ lo, y ^ hi), device_id(z, y, x, k)))
                    elif hi or lo:
                        perm.append((device_id(z, y ^ hi, x ^ lo, k), device_id(z, y, x, k)))
    return perm


def split(x):
    high = x.astype(jnp.bfloat16)
    return high, (x - high.astype(jnp.float32)).astype(jnp.bfloat16)


def dot(left, right, dims):
    return lax.dot_general(left, right, (dims, ((), ())), preferred_element_type=jnp.float32)


def dot_split(left, right, dims):
    (lh, ll), (rh, rl) = left, right
    return dot(lh, rh, dims) + dot(lh, rl, dims) + dot(ll, rh, dims)


ROWS = ((1,), (1,))
COLS = ((1,), (0,))
FLAGS = pl.BlockSpec(memory_space=pltpu.SMEM)


def room(args, outs, scratch=0):
    total = sum(math.prod(a.shape) * a.dtype.itemsize for a in (*args, *outs)) + scratch
    return pltpu.CompilerParams(vmem_limit_bytes=total + total // 4 + (6 << 20))


def call(kernel, flags, args, outs):
    outs = [jax.ShapeDtypeStruct(o, jnp.float32) for o in outs]
    whole = pl.BlockSpec(memory_space=pltpu.VMEM)
    return pl.pallas_call(
        kernel,
        out_shape=outs,
        in_specs=[FLAGS] + [whole] * len(args),
        out_specs=[whole] * len(outs),
        compiler_params=room(args, outs),
        cost_estimate=LIGHT,
    )(flags, *args)


def mine(flags_ref, side, half):
    k = flags_ref[0]
    return pl.ds(pl.multiple_of((k if side == 0 else 1 - k) * half, half), half)


def own_gram(flags, student):
    half = student.shape[0] // 2

    def kernel(flags_ref, student_ref, *outs):
        left = split(student_ref[mine(flags_ref, 0, half), :])
        right = split(student_ref[mine(flags_ref, 1, half), :])
        outs[0][...] = dot_split(left, left, ROWS)
        outs[1][...] = dot_split(left, right, ROWS)

    return call(kernel, flags, [student], [(half, half)] * 2)


def gram_part(flags, own, pair):
    half = own.shape[0]

    def kernel(flags_ref, own_ref, first_ref, second_ref, *outs):
        left = split(own_ref[...])
        for ref, out_ref in zip((first_ref, second_ref), outs):
            out_ref[...] = dot_split(left, split(ref[...]), ROWS)

    return call(kernel, flags, [own, *pair], [(half, half)] * 2)


def summed(refs, side):
    return refs[2 * side][...] + refs[2 * side + 1][...]


def teacher_parts(flags, teacher, others, keep_split=False):
    rows, width = teacher[0].shape
    half = rows // 2
    flat = [array for other in others for array in (other if isinstance(other, tuple) else (other,))]
    n = sum((other[0] if isinstance(other, tuple) else other).shape[0] for other in others)
    step = width // 4

    def kernel(flags_ref, *refs):
        teacher_refs, other_refs = refs[: len(teacher)], refs[len(teacher) :][: len(flat)]
        outs = refs[len(teacher) + len(flat) :]
        edge = flags_ref[1] == 1
        for i in range(4):
            at = slice(i * step, (i + 1) * step)
            taken = iter(other_refs)
            right = []
            for other in others:
                value = next(taken)[:, at]
                if isinstance(other, tuple):
                    value = jnp.where(edge, value, next(taken)[:, at])
                right.append(value)
            high, low = split(right[0] if len(right) == 1 else jnp.concatenate(right, 0))
            both = jnp.concatenate([high, low], 0)
            for out_ref, which in ((outs[1], 1 - flags_ref[0]), (outs[0], flags_ref[0])):
                mine = pl.ds(pl.multiple_of(which * half, half), half)
                if len(teacher) == 1:
                    th, tl = split(teacher_refs[0][mine, at])
                    if keep_split:
                        outs[2][mine, at], outs[3][mine, at] = th, tl
                else:
                    th, tl = (ref[mine, at] for ref in teacher_refs)
                part = dot(th, both, ROWS)
                part = part[:, :n] + part[:, n:] + dot(tl, high, ROWS)
                if i == 0:
                    out_ref[...] = part
                else:
                    out_ref[...] += part

    whole = pl.BlockSpec(memory_space=pltpu.VMEM)
    outs = [jax.ShapeDtypeStruct((half, n), jnp.float32)] * 2
    if keep_split:
        outs += [jax.ShapeDtypeStruct((rows, width), jnp.bfloat16)] * 2
    return pl.pallas_call(
        kernel,
        out_shape=outs,
        in_specs=[FLAGS] + [whole] * (len(teacher) + len(flat)),
        out_specs=[whole] * len(outs),
        compiler_params=room([*teacher, *flat], outs),
        cost_estimate=LIGHT,
    )(flags, *teacher, *flat)


def ordered(flags_ref, pieces):
    lo, hi = flags_ref[2] == 1, flags_ref[3] == 1
    g00, g01, g10, g11 = pieces
    a0, a1 = jnp.where(lo, g01, g00), jnp.where(lo, g00, g01)
    b0, b1 = jnp.where(lo, g11, g10), jnp.where(lo, g10, g11)
    low, high = jnp.concatenate([a0, a1], 1), jnp.concatenate([b0, b1], 1)
    return jnp.where(hi, high, low), jnp.where(hi, low, high)


def returned(flags_ref, pieces):
    edge = flags_ref[1] == 1
    left, right = ordered(flags_ref, [jnp.where(edge, pieces[4], pieces[0]), *pieces[1:4]])
    return jnp.where(edge, left.T, left), jnp.where(edge, right.T, right)


def spread(sum_ref, hsic, gram):
    row = lax.broadcasted_iota(jnp.int32, sum_ref.shape, 0)
    return jnp.where(row < 4, hsic, gram)


def products_call(kernel, flags, args, out, scratch):
    outs = [jax.ShapeDtypeStruct(shape, jnp.float32) for shape in (out, (8, 128))]
    whole = pl.BlockSpec(memory_space=pltpu.VMEM)
    return pl.pallas_call(
        kernel,
        out_shape=outs,
        in_specs=[FLAGS] + [whole] * len(args),
        out_specs=[whole] * 2,
        scratch_shapes=[pltpu.VMEM(scratch, jnp.bfloat16)] * 2,
        compiler_params=room(args, outs, 4 * math.prod(scratch)),
        cost_estimate=LIGHT,
    )(flags, *args)


def first_products(flags, pieces, ks, student, s_a):
    half, width = s_a[0].shape
    chunk = width // 4

    def kernel(flags_ref, *refs):
        tops = ordered(flags_ref, [ref[...] for ref in refs[:4]])
        ks_refs, (student_ref, left_ref, right_ref) = (refs[4:8], refs[8:12]), refs[12:15]
        out_ref, sum_ref, high, low = refs[15:]
        hsic = gram = jnp.zeros((1, 1), jnp.float32)
        for g in range(2):
            for side in range(2):
                at = slice((2 * g + side) * half, (2 * g + side + 1) * half)
                bottom = summed(ks_refs[g], side)
                high[half:, at], low[half:, at] = split(bottom)
                gram = gram + jnp.sum(bottom * bottom, keepdims=True)
                if g == 0:
                    high[:half, at], low[:half, at] = split(tops[side])
                    hsic = hsic + jnp.sum(tops[side] * bottom, keepdims=True)
        sum_ref[...] = spread(sum_ref, hsic, gram)
        for j in range(4):
            cols = slice(j * chunk, (j + 1) * chunk)
            both, lower = 0.0, 0.0
            for side in range(2):
                at = slice(side * half, (side + 1) * half)
                own = split(student_ref[mine(flags_ref, side, half), cols])
                both = both + dot_split((high[:, at], low[:, at]), own, COLS)
                at = slice((2 + side) * half, (3 + side) * half)
                a = split((left_ref, right_ref)[side][:, cols])
                lower = lower + dot_split((high[half:, at], low[half:, at]), a, COLS)
            out_ref[:half, cols] = both[:half]
            out_ref[half:, cols] = both[half:] + lower

    args = [*pieces, *[part for terms in ks for part in terms], student, *s_a]
    return products_call(kernel, flags, args, [2 * half, width], [2 * half, 4 * half])


def second_products(flags, pieces, ks, s, products, sums):
    half, width = s[0].shape
    chunk = width // 4

    def kernel(flags_ref, *refs):
        tops, refs = returned(flags_ref, [ref[...] for ref in refs[:5]]), refs[5:]
        ks_refs, s_refs, (prod_ref, before_ref) = (refs[:4], refs[4:8], refs[8:12]), refs[12:18], refs[18:20]
        out_ref, sum_ref, high, low = refs[20:]
        hsic = gram = jnp.zeros((1, 1), jnp.float32)
        for g in range(3):
            for side in range(2):
                at = slice((2 * g + side) * half, (2 * g + side + 1) * half)
                bottom = summed(ks_refs[g], side)
                if g == 0:
                    high[:, at], low[:, at] = split(tops[side])
                    hsic = hsic + jnp.sum(tops[side] * bottom, keepdims=True)
                else:
                    high[:, at], low[:, at] = split(bottom)
                    gram = gram + jnp.sum(bottom * bottom, keepdims=True)
        sum_ref[...] = before_ref[...] + spread(sum_ref, hsic, gram)
        for j in range(4):
            cols = slice(j * chunk, (j + 1) * chunk)
            upper, lower = prod_ref[:half, cols], prod_ref[half:, cols]
            for i, ref in enumerate(s_refs):
                at = slice(i * half, (i + 1) * half)
                part = dot_split((high[:, at], low[:, at]), split(ref[:, cols]), COLS)
                if i < 2:
                    upper = upper + part
                else:
                    lower = lower + part
            out_ref[:half, cols] = upper
            out_ref[half:, cols] = lower

    args = [*pieces, *[part for terms in ks for part in terms], *s, products, sums]
    return products_call(kernel, flags, args, [2 * half, width], [half, 6 * half])


def last_sums(flags, second, third, ks_b, ks_c, sums):
    half = third[0].shape[0]

    def kernel(flags_ref, *refs):
        edge = flags_ref[1] == 1
        two = returned(flags_ref, [ref[...] for ref in refs[:5]])
        three = ordered(flags_ref, [ref[...] for ref in refs[5:9]])
        b_refs, c_refs, sum_ref, outs = refs[9:13], refs[13:17], refs[17], refs[18:]
        hsic = jnp.zeros((1, 1), jnp.float32)
        for side in range(2):
            top_b = jnp.where(edge, two[side], three[side])
            top_c = jnp.where(edge, three[side], two[side])
            outs[side][...], outs[2 + side][...] = top_b, top_c
            both = top_b * summed(b_refs, side) + top_c * summed(c_refs, side)
            hsic = hsic + jnp.sum(both, keepdims=True)
        outs[4][...] = sum_ref[...] + spread(outs[4], hsic, 0.0)

    return call(kernel, flags, [*second, *third, *ks_b, *ks_c, sums], [(half, half)] * 4 + [(8, 128)])


def last_products(flags, kt, s, products):
    half, width = s[0].shape
    chunk = width // 4

    def kernel(flags_ref, *refs):
        left = [split(ref[...]) for ref in refs[:4]]
        s_refs, prod_ref, out_ref = refs[4:8], refs[8], refs[9]
        for j in range(4):
            cols = slice(j * chunk, (j + 1) * chunk)
            total = prod_ref[:half, cols]
            for part, ref in zip(left, s_refs):
                total = total + dot_split(part, split(ref[:, cols]), COLS)
            out_ref[:, cols] = total

    return call(kernel, flags, [*kt, *s, products], [(half, width)])[0]


def finish(flags, upper, products, sums, norm, scale):
    half, width = upper.shape

    def kernel(flags_ref, up_ref, prod_ref, norm_ref, *refs):
        total = sum(ref[...] for ref in refs[:-1])
        hsic, gram = total[0:1, 0:1], total[4:5, 0:1]
        factor = scale / (jnp.sqrt(gram) * norm_ref[0:1, 0:1])
        refs[-1][...] = factor * (up_ref[...] - (hsic / gram) * prod_ref[half:, :])

    return call(kernel, flags, [upper, products, norm, *sums], [(half, width)])[0]


def token_form(student, teacher, teacher_norm):
    z = lax.axis_index("tok")
    c = lax.axis_index("scol")
    k = lax.axis_index("tcol")
    rows = student.shape[0]
    half = rows // 2
    quarter = rows // 4
    tokens_all = rows * lax.axis_size("tok")
    features = student.shape[1] * lax.axis_size("scol")
    edge = jnp.logical_or(z == 0, z == 3)
    flags = jnp.stack([k, edge.astype(jnp.int32), c % 2, (c // 2 != k).astype(jnp.int32)])
    step = lax.optimization_barrier

    def send(x, perm):
        return lax.ppermute(x, "tok", perm)

    def both_halves(mine):
        return mine, lax.ppermute(mine, "tcol", CORES)

    def sum_x_y(left, right):
        left = left + lax.ppermute(left, "scol", chip_shift(1))
        right = right + lax.ppermute(right, "scol", chip_shift(2))
        return left, right

    def terms_y_x(left, right):
        return [
            left,
            lax.ppermute(left, "scol", chip_shift(2)),
            right,
            lax.ppermute(right, "scol", chip_shift(1)),
        ]

    def chip_sum(parts):
        return terms_y_x(*sum_x_y(*parts))

    def swap_rows(kept, away):
        return kept + lax.ppermute(away, "tcol", CORES)

    def same_plane(piece):
        return [piece] + [lax.ppermute(piece, "scol", chip_shift(s)) for s in (1, 2, 3)]

    def mixed(piece):
        return [piece] + [
            lax.ppermute(piece, PLANE, piece_shift(hi, lo)) for hi, lo in ((0, 1), (1, 0), (1, 1), (0, 0))
        ]

    s_half = lax.dynamic_slice_in_dim(student, k * half, half, 0)
    near, mid = send(s_half, PAIRS), send(s_half, MIDDLE)
    ks_own = chip_sum(own_gram(flags, student))
    t_quarter = lax.dynamic_slice_in_dim(teacher, c * quarter, quarter, 0)
    kept, away, *t_split = teacher_parts(flags, [teacher], [t_quarter], True)
    own = swap_rows(kept, away)
    near, mid, t_quarter, ks_own, own, t_split = step((near, mid, t_quarter, ks_own, own, t_split))

    far_edge, far_mid = send(mid, OUTWARD), send(near, MIDDLE)
    t_in = send(t_quarter, INWARD)
    pieces_own = same_plane(own)
    s_a = both_halves(near)
    part_a = sum_x_y(*gram_part(flags, s_half, s_a))
    far_edge, far_mid, t_in, mid, t_quarter, s_a, part_a, pieces_own = step(
        (far_edge, far_mid, t_in, mid, t_quarter, s_a, part_a, pieces_own)
    )

    last_edge, t_cross = send(far_mid, OUTWARD), send(t_in, MIDDLE)
    ks_a = terms_y_x(*part_a)
    s_b = both_halves(jnp.where(edge, far_edge, mid))
    first = swap_rows(*teacher_parts(flags, t_split, [t_in]))
    back_in = send(first, OUTWARD)
    ks_b = chip_sum(gram_part(flags, s_half, s_b))
    products, sums = first_products(flags, pieces_own, [ks_own, ks_a], student, s_a)
    t_cross, far_mid, t_quarter, s_b, first, back_in, ks_b, products, sums = step(
        (t_cross, far_mid, t_quarter, s_b, first, back_in, ks_b, products, sums)
    )

    t_edge, t_mid = send(t_cross, OUTWARD), send(t_quarter, MIDDLE)
    pieces_first = mixed(jnp.where(edge, back_in, first))
    s_c = both_halves(jnp.where(edge, last_edge, far_mid))
    part_c = sum_x_y(*gram_part(flags, s_half, s_c))
    pieces_first, part_c, t_cross = step((pieces_first, part_c, t_cross))
    cross = swap_rows(*teacher_parts(flags, t_split, [t_cross]))
    back_cross = send(cross, FAR)
    ks_c = terms_y_x(*part_c)
    t_edge, t_mid, cross = step((t_edge, t_mid, cross))

    pieces_third = same_plane(swap_rows(*teacher_parts(flags, t_split, [(t_edge, t_mid)])))
    pieces_second = mixed(jnp.where(edge, back_cross, cross))
    s_abc = [*s_a, *s_b, *s_c]
    products, sums = second_products(flags, pieces_first, [ks_a, ks_b, ks_c], s_abc, products, sums)
    *kt_bc, sums = last_sums(flags, pieces_second, pieces_third, ks_b, ks_c, sums)
    sums = sums + lax.ppermute(sums, "tcol", CORES)
    planes = [sums] + [lax.ppermute(sums, "tok", [(i, (i + s) % 4) for i in range(4)]) for s in (1, 2, 3)]
    upper = last_products(flags, kt_bc, [*s_b, *s_c], products)
    scale = -2.0 * tokens_all * features
    return finish(flags, upper, products, planes, teacher_norm.reshape(1, 1), scale)


def solution(mesh):
    sizes = (mesh.shape["tok"], mesh.shape["scol"], mesh.shape["tcol"])

    def body(student, teacher, teacher_norm):
        tokens_all = student.shape[0] * sizes[0]
        features = student.shape[1] * sizes[1]
        if sizes == (4, 4, 2) and tokens_all <= features:
            return token_form(student, teacher, teacher_norm)
        return feature_form(student, teacher, teacher_norm)

    return jax.shard_map(
        body,
        mesh=mesh,
        in_specs=(P("tok", "scol"), P("tok", "tcol"), P()),
        out_specs=P(("tok", "tcol"), "scol"),
        check_vma=False,
    )
```

```python
import math

import jax
import jax.numpy as jnp
from jax import lax
from jax.experimental import pallas as pl
from jax.experimental.pallas import tpu as pltpu
from jax.sharding import PartitionSpec as P

LIGHT = pl.CostEstimate(flops=0, bytes_accessed=0, transcendentals=0)
PLANE = ("tok", "scol", "tcol")


def token_contract(left, right):
    return lax.dot_general(
        left,
        right,
        (((0,), (0,)), ((), ())),
        precision=lax.Precision.HIGHEST,
        preferred_element_type=jnp.float32,
    )


def feature_contract(left, right):
    return lax.dot_general(
        left,
        right,
        (((1,), (1,)), ((), ())),
        precision=lax.Precision.HIGHEST,
        preferred_element_type=jnp.float32,
    )


def feature_form(student, teacher, teacher_norm):
    col_index = lax.axis_index("tcol")
    tcol_count = lax.axis_size("tcol")
    tok_rows = student.shape[0]
    local_width = student.shape[1]
    features = local_width * lax.axis_size("scol")
    part_width = local_width // tcol_count
    own_slice = lax.dynamic_slice_in_dim(student, col_index * part_width, part_width, 1)
    partner = lax.all_gather(own_slice, "scol", axis=1, tiled=True)
    cov_block = token_contract(student, teacher)
    gram_block = token_contract(student, partner)
    cov_block, gram_block = lax.psum((cov_block, gram_block), "tok")
    local_stats = jnp.stack([jnp.sum(cov_block * cov_block), jnp.sum(gram_block * gram_block)])
    gathered = lax.all_gather(local_stats, ("scol", "tcol"), axis=0, tiled=True)
    totals = jnp.sum(gathered.reshape(-1, 2), axis=0)
    tokens_all = tok_rows * lax.axis_size("tok")
    factor = -2.0 * tokens_all * features / (jnp.sqrt(totals[1]) * teacher_norm[0])
    gram_ratio = totals[0] / totals[1]
    result = feature_contract(teacher, cov_block) - gram_ratio * feature_contract(
        partner, gram_block
    )
    return lax.psum_scatter(factor * result, "tcol", scatter_dimension=0, tiled=True)


PAIRS = [(0, 1), (1, 0), (2, 3), (3, 2)]
MIDDLE = [(1, 2), (2, 1)]
OUTWARD = [(1, 0), (2, 3)]
INWARD = [(0, 1), (3, 2)]
FAR = [(2, 0), (1, 3)]
CORES = [(0, 1), (1, 0)]


def chip_shift(shift):
    return [(c, c ^ shift) for c in range(4)]


def device_id(z, y, x, k):
    return ((z * 2 + y) * 2 + x) * 2 + k


def piece_shift(hi, lo):
    perm = []
    for z in range(4):
        for y in range(2):
            for x in range(2):
                for k in range(2):
                    if z in (0, 3):
                        perm.append((device_id(z, k, x ^ lo, y ^ hi), device_id(z, y, x, k)))
                    elif hi or lo:
                        perm.append((device_id(z, y ^ hi, x ^ lo, k), device_id(z, y, x, k)))
    return perm


def split(x):
    high = x.astype(jnp.bfloat16)
    return high, (x - high.astype(jnp.float32)).astype(jnp.bfloat16)


def dot(left, right, dims):
    return lax.dot_general(left, right, (dims, ((), ())), preferred_element_type=jnp.float32)


def dot_split(left, right, dims):
    (lh, ll), (rh, rl) = left, right
    return dot(lh, rh, dims) + dot(lh, rl, dims) + dot(ll, rh, dims)


ROWS = ((1,), (1,))
COLS = ((1,), (0,))
FLAGS = pl.BlockSpec(memory_space=pltpu.SMEM)


def room(args, outs, scratch=0):
    total = sum(math.prod(a.shape) * a.dtype.itemsize for a in (*args, *outs)) + scratch
    return pltpu.CompilerParams(vmem_limit_bytes=total + total // 4 + (6 << 20))


def call(kernel, flags, args, outs):
    outs = [jax.ShapeDtypeStruct(o, jnp.float32) for o in outs]
    whole = pl.BlockSpec(memory_space=pltpu.VMEM)
    return pl.pallas_call(
        kernel,
        out_shape=outs,
        in_specs=[FLAGS] + [whole] * len(args),
        out_specs=[whole] * len(outs),
        compiler_params=room(args, outs),
        cost_estimate=LIGHT,
    )(flags, *args)


def mine(flags_ref, side, half):
    k = flags_ref[0]
    return pl.ds(pl.multiple_of((k if side == 0 else 1 - k) * half, half), half)


def own_gram(flags, student):
    half = student.shape[0] // 2

    def kernel(flags_ref, student_ref, *outs):
        left = split(student_ref[mine(flags_ref, 0, half), :])
        right = split(student_ref[mine(flags_ref, 1, half), :])
        outs[0][...] = dot_split(left, left, ROWS)
        outs[1][...] = dot_split(left, right, ROWS)

    return call(kernel, flags, [student], [(half, half)] * 2)


def gram_part(flags, own, pair):
    half = own.shape[0]

    def kernel(flags_ref, own_ref, first_ref, second_ref, *outs):
        left = split(own_ref[...])
        for ref, out_ref in zip((first_ref, second_ref), outs):
            out_ref[...] = dot_split(left, split(ref[...]), ROWS)

    return call(kernel, flags, [own, *pair], [(half, half)] * 2)


def summed(refs, side):
    return refs[2 * side][...] + refs[2 * side + 1][...]


def teacher_parts(flags, teacher, others, keep_split=False):
    rows, width = teacher[0].shape
    half = rows // 2
    flat = [array for other in others for array in (other if isinstance(other, tuple) else (other,))]
    n = sum((other[0] if isinstance(other, tuple) else other).shape[0] for other in others)
    step = width // 4

    def kernel(flags_ref, *refs):
        teacher_refs, other_refs = refs[: len(teacher)], refs[len(teacher) :][: len(flat)]
        outs = refs[len(teacher) + len(flat) :]
        edge = flags_ref[1] == 1
        for i in range(4):
            at = slice(i * step, (i + 1) * step)
            taken = iter(other_refs)
            right = []
            for other in others:
                value = next(taken)[:, at]
                if isinstance(other, tuple):
                    value = jnp.where(edge, value, next(taken)[:, at])
                right.append(value)
            high, low = split(right[0] if len(right) == 1 else jnp.concatenate(right, 0))
            both = jnp.concatenate([high, low], 0)
            for out_ref, which in ((outs[1], 1 - flags_ref[0]), (outs[0], flags_ref[0])):
                mine = pl.ds(pl.multiple_of(which * half, half), half)
                if len(teacher) == 1:
                    th, tl = split(teacher_refs[0][mine, at])
                    if keep_split:
                        outs[2][mine, at], outs[3][mine, at] = th, tl
                else:
                    th, tl = (ref[mine, at] for ref in teacher_refs)
                part = dot(th, both, ROWS)
                part = part[:, :n] + part[:, n:] + dot(tl, high, ROWS)
                if i == 0:
                    out_ref[...] = part
                else:
                    out_ref[...] += part

    whole = pl.BlockSpec(memory_space=pltpu.VMEM)
    outs = [jax.ShapeDtypeStruct((half, n), jnp.float32)] * 2
    if keep_split:
        outs += [jax.ShapeDtypeStruct((rows, width), jnp.bfloat16)] * 2
    return pl.pallas_call(
        kernel,
        out_shape=outs,
        in_specs=[FLAGS] + [whole] * (len(teacher) + len(flat)),
        out_specs=[whole] * len(outs),
        compiler_params=room([*teacher, *flat], outs),
        cost_estimate=LIGHT,
    )(flags, *teacher, *flat)


def ordered(flags_ref, pieces):
    lo, hi = flags_ref[2] == 1, flags_ref[3] == 1
    g00, g01, g10, g11 = pieces
    a0, a1 = jnp.where(lo, g01, g00), jnp.where(lo, g00, g01)
    b0, b1 = jnp.where(lo, g11, g10), jnp.where(lo, g10, g11)
    low, high = jnp.concatenate([a0, a1], 1), jnp.concatenate([b0, b1], 1)
    return jnp.where(hi, high, low), jnp.where(hi, low, high)


def returned(flags_ref, pieces):
    edge = flags_ref[1] == 1
    left, right = ordered(flags_ref, [jnp.where(edge, pieces[4], pieces[0]), *pieces[1:4]])
    return jnp.where(edge, left.T, left), jnp.where(edge, right.T, right)


def spread(sum_ref, hsic, gram):
    row = lax.broadcasted_iota(jnp.int32, sum_ref.shape, 0)
    return jnp.where(row < 4, hsic, gram)


def products_call(kernel, flags, args, out, scratch):
    outs = [jax.ShapeDtypeStruct(shape, jnp.float32) for shape in (out, (8, 128))]
    whole = pl.BlockSpec(memory_space=pltpu.VMEM)
    return pl.pallas_call(
        kernel,
        out_shape=outs,
        in_specs=[FLAGS] + [whole] * len(args),
        out_specs=[whole] * 2,
        scratch_shapes=[pltpu.VMEM(scratch, jnp.bfloat16)] * 2,
        compiler_params=room(args, outs, 4 * math.prod(scratch)),
        cost_estimate=LIGHT,
    )(flags, *args)


def first_products(flags, pieces, ks, student, s_a):
    half, width = s_a[0].shape
    chunk = width // 4

    def kernel(flags_ref, *refs):
        tops = ordered(flags_ref, [ref[...] for ref in refs[:4]])
        ks_refs, (student_ref, left_ref, right_ref) = (refs[4:8], refs[8:12]), refs[12:15]
        out_ref, sum_ref, high, low = refs[15:]
        hsic = gram = jnp.zeros((1, 1), jnp.float32)
        for g in range(2):
            for side in range(2):
                at = slice((2 * g + side) * half, (2 * g + side + 1) * half)
                bottom = summed(ks_refs[g], side)
                high[half:, at], low[half:, at] = split(bottom)
                gram = gram + jnp.sum(bottom * bottom, keepdims=True)
                if g == 0:
                    high[:half, at], low[:half, at] = split(tops[side])
                    hsic = hsic + jnp.sum(tops[side] * bottom, keepdims=True)
        sum_ref[...] = spread(sum_ref, hsic, gram)
        for j in range(4):
            cols = slice(j * chunk, (j + 1) * chunk)
            both, lower = 0.0, 0.0
            for side in range(2):
                at = slice(side * half, (side + 1) * half)
                own = split(student_ref[mine(flags_ref, side, half), cols])
                both = both + dot_split((high[:, at], low[:, at]), own, COLS)
                at = slice((2 + side) * half, (3 + side) * half)
                a = split((left_ref, right_ref)[side][:, cols])
                lower = lower + dot_split((high[half:, at], low[half:, at]), a, COLS)
            out_ref[:half, cols] = both[:half]
            out_ref[half:, cols] = both[half:] + lower

    args = [*pieces, *[part for terms in ks for part in terms], student, *s_a]
    return products_call(kernel, flags, args, [2 * half, width], [2 * half, 4 * half])


def second_products(flags, pieces, ks, s, products, sums):
    half, width = s[0].shape
    chunk = width // 4

    def kernel(flags_ref, *refs):
        tops, refs = returned(flags_ref, [ref[...] for ref in refs[:5]]), refs[5:]
        ks_refs, s_refs, (prod_ref, before_ref) = (refs[:4], refs[4:8], refs[8:12]), refs[12:18], refs[18:20]
        out_ref, sum_ref, high, low = refs[20:]
        hsic = gram = jnp.zeros((1, 1), jnp.float32)
        for g in range(3):
            for side in range(2):
                at = slice((2 * g + side) * half, (2 * g + side + 1) * half)
                bottom = summed(ks_refs[g], side)
                if g == 0:
                    high[:, at], low[:, at] = split(tops[side])
                    hsic = hsic + jnp.sum(tops[side] * bottom, keepdims=True)
                else:
                    high[:, at], low[:, at] = split(bottom)
                    gram = gram + jnp.sum(bottom * bottom, keepdims=True)
        sum_ref[...] = before_ref[...] + spread(sum_ref, hsic, gram)
        for j in range(4):
            cols = slice(j * chunk, (j + 1) * chunk)
            upper, lower = prod_ref[:half, cols], prod_ref[half:, cols]
            for i, ref in enumerate(s_refs):
                at = slice(i * half, (i + 1) * half)
                part = dot_split((high[:, at], low[:, at]), split(ref[:, cols]), COLS)
                if i < 2:
                    upper = upper + part
                else:
                    lower = lower + part
            out_ref[:half, cols] = upper
            out_ref[half:, cols] = lower

    args = [*pieces, *[part for terms in ks for part in terms], *s, products, sums]
    return products_call(kernel, flags, args, [2 * half, width], [half, 6 * half])


def last_sums(flags, second, third, ks_b, ks_c, sums):
    half = third[0].shape[0]

    def kernel(flags_ref, *refs):
        edge = flags_ref[1] == 1
        two = returned(flags_ref, [ref[...] for ref in refs[:5]])
        three = ordered(flags_ref, [ref[...] for ref in refs[5:9]])
        b_refs, c_refs, sum_ref, outs = refs[9:13], refs[13:17], refs[17], refs[18:]
        hsic = jnp.zeros((1, 1), jnp.float32)
        for side in range(2):
            top_b = jnp.where(edge, two[side], three[side])
            top_c = jnp.where(edge, three[side], two[side])
            outs[side][...], outs[2 + side][...] = top_b, top_c
            both = top_b * summed(b_refs, side) + top_c * summed(c_refs, side)
            hsic = hsic + jnp.sum(both, keepdims=True)
        outs[4][...] = sum_ref[...] + spread(outs[4], hsic, 0.0)

    return call(kernel, flags, [*second, *third, *ks_b, *ks_c, sums], [(half, half)] * 4 + [(8, 128)])


def last_products(flags, kt, s, products):
    half, width = s[0].shape
    chunk = width // 4

    def kernel(flags_ref, *refs):
        left = [split(ref[...]) for ref in refs[:4]]
        s_refs, prod_ref, out_ref = refs[4:8], refs[8], refs[9]
        for j in range(4):
            cols = slice(j * chunk, (j + 1) * chunk)
            total = prod_ref[:half, cols]
            for part, ref in zip(left, s_refs):
                total = total + dot_split(part, split(ref[:, cols]), COLS)
            out_ref[:, cols] = total

    return call(kernel, flags, [*kt, *s, products], [(half, width)])[0]


def finish(flags, upper, products, sums, norm, scale):
    half, width = upper.shape

    def kernel(flags_ref, up_ref, prod_ref, norm_ref, *refs):
        total = sum(ref[...] for ref in refs[:-1])
        hsic, gram = total[0:1, 0:1], total[4:5, 0:1]
        factor = scale / (jnp.sqrt(gram) * norm_ref[0:1, 0:1])
        refs[-1][...] = factor * (up_ref[...] - (hsic / gram) * prod_ref[half:, :])

    return call(kernel, flags, [upper, products, norm, *sums], [(half, width)])[0]


def token_form(student, teacher, teacher_norm):
    z = lax.axis_index("tok")
    c = lax.axis_index("scol")
    k = lax.axis_index("tcol")
    rows = student.shape[0]
    half = rows // 2
    quarter = rows // 4
    tokens_all = rows * lax.axis_size("tok")
    features = student.shape[1] * lax.axis_size("scol")
    edge = jnp.logical_or(z == 0, z == 3)
    flags = jnp.stack([k, edge.astype(jnp.int32), c % 2, (c // 2 != k).astype(jnp.int32)])
    step = lax.optimization_barrier

    def send(x, perm):
        return lax.ppermute(x, "tok", perm)

    def both_halves(mine):
        return mine, lax.ppermute(mine, "tcol", CORES)

    def sum_x_y(left, right):
        left = left + lax.ppermute(left, "scol", chip_shift(1))
        right = right + lax.ppermute(right, "scol", chip_shift(2))
        return left, right

    def terms_y_x(left, right):
        return [
            left,
            lax.ppermute(left, "scol", chip_shift(2)),
            right,
            lax.ppermute(right, "scol", chip_shift(1)),
        ]

    def chip_sum(parts):
        return terms_y_x(*sum_x_y(*parts))

    def swap_rows(kept, away):
        return kept + lax.ppermute(away, "tcol", CORES)

    def same_plane(piece):
        return [piece] + [lax.ppermute(piece, "scol", chip_shift(s)) for s in (1, 2, 3)]

    def mixed(piece):
        return [piece] + [
            lax.ppermute(piece, PLANE, piece_shift(hi, lo)) for hi, lo in ((0, 1), (1, 0), (1, 1), (0, 0))
        ]

    s_half = lax.dynamic_slice_in_dim(student, k * half, half, 0)
    near, mid = send(s_half, PAIRS), send(s_half, MIDDLE)
    ks_own = chip_sum(own_gram(flags, student))
    t_quarter = lax.dynamic_slice_in_dim(teacher, c * quarter, quarter, 0)
    kept, away, *t_split = teacher_parts(flags, [teacher], [t_quarter], True)
    own = swap_rows(kept, away)
    near, mid, t_quarter, ks_own, own, t_split = step((near, mid, t_quarter, ks_own, own, t_split))

    far_edge, far_mid = send(mid, OUTWARD), send(near, MIDDLE)
    t_in = send(t_quarter, INWARD)
    pieces_own = same_plane(own)
    s_a = both_halves(near)
    part_a = sum_x_y(*gram_part(flags, s_half, s_a))
    far_edge, far_mid, t_in, mid, t_quarter, s_a, part_a, pieces_own = step(
        (far_edge, far_mid, t_in, mid, t_quarter, s_a, part_a, pieces_own)
    )

    last_edge, t_cross = send(far_mid, OUTWARD), send(t_in, MIDDLE)
    ks_a = terms_y_x(*part_a)
    s_b = both_halves(jnp.where(edge, far_edge, mid))
    first = swap_rows(*teacher_parts(flags, t_split, [t_in]))
    back_in = send(first, OUTWARD)
    ks_b = chip_sum(gram_part(flags, s_half, s_b))
    products, sums = first_products(flags, pieces_own, [ks_own, ks_a], student, s_a)
    t_cross, far_mid, t_quarter, s_b, first, back_in, ks_b, products, sums = step(
        (t_cross, far_mid, t_quarter, s_b, first, back_in, ks_b, products, sums)
    )

    t_edge, t_mid = send(t_cross, OUTWARD), send(t_quarter, MIDDLE)
    pieces_first = mixed(jnp.where(edge, back_in, first))
    s_c = both_halves(jnp.where(edge, last_edge, far_mid))
    part_c = sum_x_y(*gram_part(flags, s_half, s_c))
    part_c, t_cross = step((part_c, t_cross))
    cross = swap_rows(*teacher_parts(flags, t_split, [t_cross]))
    back_cross = send(cross, FAR)
    ks_c = terms_y_x(*part_c)
    t_edge, t_mid, cross, pieces_first = step((t_edge, t_mid, cross, pieces_first))

    pieces_third = same_plane(swap_rows(*teacher_parts(flags, t_split, [(t_edge, t_mid)])))
    pieces_second = mixed(jnp.where(edge, back_cross, cross))
    s_abc = [*s_a, *s_b, *s_c]
    products, sums = second_products(flags, pieces_first, [ks_a, ks_b, ks_c], s_abc, products, sums)
    *kt_bc, sums = last_sums(flags, pieces_second, pieces_third, ks_b, ks_c, sums)
    sums = sums + lax.ppermute(sums, "tcol", CORES)
    planes = [sums] + [lax.ppermute(sums, "tok", [(i, (i + s) % 4) for i in range(4)]) for s in (1, 2, 3)]
    upper = last_products(flags, kt_bc, [*s_b, *s_c], products)
    scale = -2.0 * tokens_all * features
    return finish(flags, upper, products, planes, teacher_norm.reshape(1, 1), scale)


def solution(mesh):
    sizes = (mesh.shape["tok"], mesh.shape["scol"], mesh.shape["tcol"])

    def body(student, teacher, teacher_norm):
        tokens_all = student.shape[0] * sizes[0]
        features = student.shape[1] * sizes[1]
        if sizes == (4, 4, 2) and tokens_all <= features:
            return token_form(student, teacher, teacher_norm)
        return feature_form(student, teacher, teacher_norm)

    return jax.shard_map(
        body,
        mesh=mesh,
        in_specs=(P("tok", "scol"), P("tok", "tcol"), P()),
        out_specs=P(("tok", "tcol"), "scol"),
        check_vma=False,
    )
```

```python
import math

import jax
import jax.numpy as jnp
from jax import lax
from jax.experimental import pallas as pl
from jax.experimental.pallas import tpu as pltpu
from jax.sharding import PartitionSpec as P

LIGHT = pl.CostEstimate(flops=0, bytes_accessed=0, transcendentals=0)
PLANE = ("tok", "scol", "tcol")


def token_contract(left, right):
    return lax.dot_general(
        left,
        right,
        (((0,), (0,)), ((), ())),
        precision=lax.Precision.HIGHEST,
        preferred_element_type=jnp.float32,
    )


def feature_contract(left, right):
    return lax.dot_general(
        left,
        right,
        (((1,), (1,)), ((), ())),
        precision=lax.Precision.HIGHEST,
        preferred_element_type=jnp.float32,
    )


def feature_form(student, teacher, teacher_norm):
    col_index = lax.axis_index("tcol")
    tcol_count = lax.axis_size("tcol")
    tok_rows = student.shape[0]
    local_width = student.shape[1]
    features = local_width * lax.axis_size("scol")
    part_width = local_width // tcol_count
    own_slice = lax.dynamic_slice_in_dim(student, col_index * part_width, part_width, 1)
    partner = lax.all_gather(own_slice, "scol", axis=1, tiled=True)
    cov_block = token_contract(student, teacher)
    gram_block = token_contract(student, partner)
    cov_block, gram_block = lax.psum((cov_block, gram_block), "tok")
    local_stats = jnp.stack([jnp.sum(cov_block * cov_block), jnp.sum(gram_block * gram_block)])
    gathered = lax.all_gather(local_stats, ("scol", "tcol"), axis=0, tiled=True)
    totals = jnp.sum(gathered.reshape(-1, 2), axis=0)
    tokens_all = tok_rows * lax.axis_size("tok")
    factor = -2.0 * tokens_all * features / (jnp.sqrt(totals[1]) * teacher_norm[0])
    gram_ratio = totals[0] / totals[1]
    result = feature_contract(teacher, cov_block) - gram_ratio * feature_contract(
        partner, gram_block
    )
    return lax.psum_scatter(factor * result, "tcol", scatter_dimension=0, tiled=True)


PAIRS = [(0, 1), (1, 0), (2, 3), (3, 2)]
MIDDLE = [(1, 2), (2, 1)]
OUTWARD = [(1, 0), (2, 3)]
INWARD = [(0, 1), (3, 2)]
FAR = [(2, 0), (1, 3)]
CORES = [(0, 1), (1, 0)]


def chip_shift(shift):
    return [(c, c ^ shift) for c in range(4)]


def device_id(z, y, x, k):
    return ((z * 2 + y) * 2 + x) * 2 + k


def piece_shift(hi, lo):
    perm = []
    for z in range(4):
        for y in range(2):
            for x in range(2):
                for k in range(2):
                    if z in (0, 3):
                        perm.append((device_id(z, k, x ^ lo, y ^ hi), device_id(z, y, x, k)))
                    elif hi or lo:
                        perm.append((device_id(z, y ^ hi, x ^ lo, k), device_id(z, y, x, k)))
    return perm


def split(x):
    high = x.astype(jnp.bfloat16)
    return high, (x - high.astype(jnp.float32)).astype(jnp.bfloat16)


def dot(left, right, dims):
    return lax.dot_general(left, right, (dims, ((), ())), preferred_element_type=jnp.float32)


def dot_split(left, right, dims):
    (lh, ll), (rh, rl) = left, right
    return dot(lh, rh, dims) + dot(lh, rl, dims) + dot(ll, rh, dims)


ROWS = ((1,), (1,))
COLS = ((1,), (0,))
FLAGS = pl.BlockSpec(memory_space=pltpu.SMEM)


def room(args, outs, scratch=0):
    total = sum(math.prod(a.shape) * a.dtype.itemsize for a in (*args, *outs)) + scratch
    return pltpu.CompilerParams(vmem_limit_bytes=total + total // 4 + (6 << 20))


def call(kernel, flags, args, outs):
    outs = [jax.ShapeDtypeStruct(o, jnp.float32) for o in outs]
    whole = pl.BlockSpec(memory_space=pltpu.VMEM)
    return pl.pallas_call(
        kernel,
        out_shape=outs,
        in_specs=[FLAGS] + [whole] * len(args),
        out_specs=[whole] * len(outs),
        compiler_params=room(args, outs),
        cost_estimate=LIGHT,
    )(flags, *args)


def mine(flags_ref, side, half):
    k = flags_ref[0]
    return pl.ds(pl.multiple_of((k if side == 0 else 1 - k) * half, half), half)


def own_gram(flags, student):
    half = student.shape[0] // 2

    def kernel(flags_ref, student_ref, *outs):
        left = split(student_ref[mine(flags_ref, 0, half), :])
        right = split(student_ref[mine(flags_ref, 1, half), :])
        outs[0][...] = dot_split(left, left, ROWS)
        outs[1][...] = dot_split(left, right, ROWS)

    return call(kernel, flags, [student], [(half, half)] * 2)


def gram_part(flags, own, pair):
    half = own.shape[0]

    def kernel(flags_ref, own_ref, first_ref, second_ref, *outs):
        left = split(own_ref[...])
        for ref, out_ref in zip((first_ref, second_ref), outs):
            out_ref[...] = dot_split(left, split(ref[...]), ROWS)

    return call(kernel, flags, [own, *pair], [(half, half)] * 2)


def summed(refs, side):
    return refs[2 * side][...] + refs[2 * side + 1][...]


def teacher_parts(flags, teacher, others, keep_split=False):
    rows, width = teacher[0].shape
    half = rows // 2
    flat = [array for other in others for array in (other if isinstance(other, tuple) else (other,))]
    n = sum((other[0] if isinstance(other, tuple) else other).shape[0] for other in others)
    step = width // 4

    def kernel(flags_ref, *refs):
        teacher_refs, other_refs = refs[: len(teacher)], refs[len(teacher) :][: len(flat)]
        outs = refs[len(teacher) + len(flat) :]
        edge = flags_ref[1] == 1
        for i in range(4):
            at = slice(i * step, (i + 1) * step)
            taken = iter(other_refs)
            right = []
            for other in others:
                value = next(taken)[:, at]
                if isinstance(other, tuple):
                    value = jnp.where(edge, value, next(taken)[:, at])
                right.append(value)
            high, low = split(right[0] if len(right) == 1 else jnp.concatenate(right, 0))
            both = jnp.concatenate([high, low], 0)
            for out_ref, which in ((outs[1], 1 - flags_ref[0]), (outs[0], flags_ref[0])):
                mine = pl.ds(pl.multiple_of(which * half, half), half)
                if len(teacher) == 1:
                    th, tl = split(teacher_refs[0][mine, at])
                    if keep_split:
                        outs[2][mine, at], outs[3][mine, at] = th, tl
                else:
                    th, tl = (ref[mine, at] for ref in teacher_refs)
                part = dot(th, both, ROWS)
                part = part[:, :n] + part[:, n:] + dot(tl, high, ROWS)
                if i == 0:
                    out_ref[...] = part
                else:
                    out_ref[...] += part

    whole = pl.BlockSpec(memory_space=pltpu.VMEM)
    outs = [jax.ShapeDtypeStruct((half, n), jnp.float32)] * 2
    if keep_split:
        outs += [jax.ShapeDtypeStruct((rows, width), jnp.bfloat16)] * 2
    return pl.pallas_call(
        kernel,
        out_shape=outs,
        in_specs=[FLAGS] + [whole] * (len(teacher) + len(flat)),
        out_specs=[whole] * len(outs),
        compiler_params=room([*teacher, *flat], outs),
        cost_estimate=LIGHT,
    )(flags, *teacher, *flat)


def ordered(flags_ref, pieces):
    lo, hi = flags_ref[2] == 1, flags_ref[3] == 1
    g00, g01, g10, g11 = pieces
    a0, a1 = jnp.where(lo, g01, g00), jnp.where(lo, g00, g01)
    b0, b1 = jnp.where(lo, g11, g10), jnp.where(lo, g10, g11)
    low, high = jnp.concatenate([a0, a1], 1), jnp.concatenate([b0, b1], 1)
    return jnp.where(hi, high, low), jnp.where(hi, low, high)


def returned(flags_ref, pieces):
    edge = flags_ref[1] == 1
    left, right = ordered(flags_ref, [jnp.where(edge, pieces[4], pieces[0]), *pieces[1:4]])
    return jnp.where(edge, left.T, left), jnp.where(edge, right.T, right)


def spread(sum_ref, hsic, gram):
    row = lax.broadcasted_iota(jnp.int32, sum_ref.shape, 0)
    return jnp.where(row < 4, hsic, gram)


def products_call(kernel, flags, args, out, scratch):
    outs = [jax.ShapeDtypeStruct(shape, jnp.float32) for shape in (out, (8, 128))]
    whole = pl.BlockSpec(memory_space=pltpu.VMEM)
    return pl.pallas_call(
        kernel,
        out_shape=outs,
        in_specs=[FLAGS] + [whole] * len(args),
        out_specs=[whole] * 2,
        scratch_shapes=[pltpu.VMEM(scratch, jnp.bfloat16)] * 2,
        compiler_params=room(args, outs, 4 * math.prod(scratch)),
        cost_estimate=LIGHT,
    )(flags, *args)


def first_products(flags, pieces, ks, student, s_a):
    half, width = s_a[0].shape
    chunk = width // 4

    def kernel(flags_ref, *refs):
        tops = ordered(flags_ref, [ref[...] for ref in refs[:4]])
        ks_refs, (student_ref, left_ref, right_ref) = (refs[4:8], refs[8:12]), refs[12:15]
        out_ref, sum_ref, high, low = refs[15:]
        hsic = gram = jnp.zeros((1, 1), jnp.float32)
        for g in range(2):
            for side in range(2):
                at = slice((2 * g + side) * half, (2 * g + side + 1) * half)
                bottom = summed(ks_refs[g], side)
                high[half:, at], low[half:, at] = split(bottom)
                gram = gram + jnp.sum(bottom * bottom, keepdims=True)
                if g == 0:
                    high[:half, at], low[:half, at] = split(tops[side])
                    hsic = hsic + jnp.sum(tops[side] * bottom, keepdims=True)
        sum_ref[...] = spread(sum_ref, hsic, gram)
        for j in range(4):
            cols = slice(j * chunk, (j + 1) * chunk)
            both, lower = 0.0, 0.0
            for side in range(2):
                at = slice(side * half, (side + 1) * half)
                own = split(student_ref[mine(flags_ref, side, half), cols])
                both = both + dot_split((high[:, at], low[:, at]), own, COLS)
                at = slice((2 + side) * half, (3 + side) * half)
                a = split((left_ref, right_ref)[side][:, cols])
                lower = lower + dot_split((high[half:, at], low[half:, at]), a, COLS)
            out_ref[:half, cols] = both[:half]
            out_ref[half:, cols] = both[half:] + lower

    args = [*pieces, *[part for terms in ks for part in terms], student, *s_a]
    return products_call(kernel, flags, args, [2 * half, width], [2 * half, 4 * half])


def second_products(flags, pieces, ks, s, products, sums):
    half, width = s[0].shape
    chunk = width // 4

    def kernel(flags_ref, *refs):
        tops, refs = returned(flags_ref, [ref[...] for ref in refs[:5]]), refs[5:]
        ks_refs, s_refs, (prod_ref, before_ref) = (refs[:4], refs[4:8], refs[8:12]), refs[12:18], refs[18:20]
        out_ref, sum_ref, high, low = refs[20:]
        hsic = gram = jnp.zeros((1, 1), jnp.float32)
        for g in range(3):
            for side in range(2):
                at = slice((2 * g + side) * half, (2 * g + side + 1) * half)
                bottom = summed(ks_refs[g], side)
                if g == 0:
                    high[:, at], low[:, at] = split(tops[side])
                    hsic = hsic + jnp.sum(tops[side] * bottom, keepdims=True)
                else:
                    high[:, at], low[:, at] = split(bottom)
                    gram = gram + jnp.sum(bottom * bottom, keepdims=True)
        sum_ref[...] = before_ref[...] + spread(sum_ref, hsic, gram)
        for j in range(4):
            cols = slice(j * chunk, (j + 1) * chunk)
            upper, lower = prod_ref[:half, cols], prod_ref[half:, cols]
            for i, ref in enumerate(s_refs):
                at = slice(i * half, (i + 1) * half)
                part = dot_split((high[:, at], low[:, at]), split(ref[:, cols]), COLS)
                if i < 2:
                    upper = upper + part
                else:
                    lower = lower + part
            out_ref[:half, cols] = upper
            out_ref[half:, cols] = lower

    args = [*pieces, *[part for terms in ks for part in terms], *s, products, sums]
    return products_call(kernel, flags, args, [2 * half, width], [half, 6 * half])


def last_sums(flags, second, third, ks_b, ks_c, sums):
    half = third[0].shape[0]

    def kernel(flags_ref, *refs):
        edge = flags_ref[1] == 1
        two = returned(flags_ref, [ref[...] for ref in refs[:5]])
        three = ordered(flags_ref, [ref[...] for ref in refs[5:9]])
        b_refs, c_refs, sum_ref, outs = refs[9:13], refs[13:17], refs[17], refs[18:]
        hsic = jnp.zeros((1, 1), jnp.float32)
        for side in range(2):
            top_b = jnp.where(edge, two[side], three[side])
            top_c = jnp.where(edge, three[side], two[side])
            outs[side][...], outs[2 + side][...] = top_b, top_c
            both = top_b * summed(b_refs, side) + top_c * summed(c_refs, side)
            hsic = hsic + jnp.sum(both, keepdims=True)
        outs[4][...] = sum_ref[...] + spread(outs[4], hsic, 0.0)

    return call(kernel, flags, [*second, *third, *ks_b, *ks_c, sums], [(half, half)] * 4 + [(8, 128)])


def last_products(flags, kt, s, products):
    half, width = s[0].shape
    chunk = width // 4

    def kernel(flags_ref, *refs):
        left = [split(ref[...]) for ref in refs[:4]]
        s_refs, prod_ref, out_ref = refs[4:8], refs[8], refs[9]
        for j in range(4):
            cols = slice(j * chunk, (j + 1) * chunk)
            total = prod_ref[:half, cols]
            for part, ref in zip(left, s_refs):
                total = total + dot_split(part, split(ref[:, cols]), COLS)
            out_ref[:, cols] = total

    return call(kernel, flags, [*kt, *s, products], [(half, width)])[0]


def finish(flags, upper, products, sums, norm, scale):
    half, width = upper.shape

    def kernel(flags_ref, up_ref, prod_ref, norm_ref, *refs):
        total = sum(ref[...] for ref in refs[:-1])
        hsic, gram = total[0:1, 0:1], total[4:5, 0:1]
        factor = scale / (jnp.sqrt(gram) * norm_ref[0:1, 0:1])
        refs[-1][...] = factor * (up_ref[...] - (hsic / gram) * prod_ref[half:, :])

    return call(kernel, flags, [upper, products, norm, *sums], [(half, width)])[0]


def token_form(student, teacher, teacher_norm):
    z = lax.axis_index("tok")
    c = lax.axis_index("scol")
    k = lax.axis_index("tcol")
    rows = student.shape[0]
    half = rows // 2
    quarter = rows // 4
    tokens_all = rows * lax.axis_size("tok")
    features = student.shape[1] * lax.axis_size("scol")
    edge = jnp.logical_or(z == 0, z == 3)
    flags = jnp.stack([k, edge.astype(jnp.int32), c % 2, (c // 2 != k).astype(jnp.int32)])
    step = lax.optimization_barrier

    def send(x, perm):
        return lax.ppermute(x, "tok", perm)

    def both_halves(mine):
        return mine, lax.ppermute(mine, "tcol", CORES)

    def sum_x_y(left, right):
        left = left + lax.ppermute(left, "scol", chip_shift(1))
        right = right + lax.ppermute(right, "scol", chip_shift(2))
        return left, right

    def terms_y_x(left, right):
        return [
            left,
            lax.ppermute(left, "scol", chip_shift(2)),
            right,
            lax.ppermute(right, "scol", chip_shift(1)),
        ]

    def chip_sum(parts):
        return terms_y_x(*sum_x_y(*parts))

    def swap_rows(kept, away):
        return kept + lax.ppermute(away, "tcol", CORES)

    def same_plane(piece):
        return [piece] + [lax.ppermute(piece, "scol", chip_shift(s)) for s in (1, 2, 3)]

    def mixed(piece):
        return [piece] + [
            lax.ppermute(piece, PLANE, piece_shift(hi, lo)) for hi, lo in ((0, 1), (1, 0), (1, 1), (0, 0))
        ]

    s_half = lax.dynamic_slice_in_dim(student, k * half, half, 0)
    near, mid = send(s_half, PAIRS), send(s_half, MIDDLE)
    ks_own = chip_sum(own_gram(flags, student))
    t_quarter = lax.dynamic_slice_in_dim(teacher, c * quarter, quarter, 0)
    kept, away, *t_split = teacher_parts(flags, [teacher], [t_quarter], True)
    own = swap_rows(kept, away)
    near, mid, t_quarter, ks_own, own, t_split = step((near, mid, t_quarter, ks_own, own, t_split))

    far_edge, far_mid = send(mid, OUTWARD), send(near, MIDDLE)
    t_in = send(t_quarter, INWARD)
    pieces_own = same_plane(own)
    s_a = both_halves(near)
    part_a = sum_x_y(*gram_part(flags, s_half, s_a))
    far_edge, far_mid, t_in, mid, t_quarter, s_a, part_a, pieces_own = step(
        (far_edge, far_mid, t_in, mid, t_quarter, s_a, part_a, pieces_own)
    )

    last_edge, t_cross = send(far_mid, OUTWARD), send(t_in, MIDDLE)
    ks_a = terms_y_x(*part_a)
    s_b = both_halves(jnp.where(edge, far_edge, mid))
    first = swap_rows(*teacher_parts(flags, t_split, [t_in]))
    back_in = send(first, OUTWARD)
    ks_b = chip_sum(gram_part(flags, s_half, s_b))
    products, sums = first_products(flags, pieces_own, [ks_own, ks_a], student, s_a)
    t_cross, far_mid, t_quarter, s_b, first, back_in, ks_b, products, sums = step(
        (t_cross, far_mid, t_quarter, s_b, first, back_in, ks_b, products, sums)
    )

    t_edge, t_mid = send(t_cross, OUTWARD), send(t_quarter, MIDDLE)
    pieces_first = mixed(jnp.where(edge, back_in, first))
    s_c = both_halves(jnp.where(edge, last_edge, far_mid))
    part_c = sum_x_y(*gram_part(flags, s_half, s_c))
    part_c, t_cross = step((part_c, t_cross))
    cross = swap_rows(*teacher_parts(flags, t_split, [t_cross]))
    back_cross = send(cross, FAR)
    ks_c = terms_y_x(*part_c)
    t_edge, t_mid, cross = step((t_edge, t_mid, cross))

    pieces_third = same_plane(swap_rows(*teacher_parts(flags, t_split, [(t_edge, t_mid)])))
    pieces_second = mixed(jnp.where(edge, back_cross, cross))
    s_abc = [*s_a, *s_b, *s_c]
    products, sums = second_products(flags, pieces_first, [ks_a, ks_b, ks_c], s_abc, products, sums)
    *kt_bc, sums = last_sums(flags, pieces_second, pieces_third, ks_b, ks_c, sums)
    sums = sums + lax.ppermute(sums, "tcol", CORES)
    planes = [sums] + [lax.ppermute(sums, "tok", [(i, (i + s) % 4) for i in range(4)]) for s in (1, 2, 3)]
    upper = last_products(flags, kt_bc, [*s_b, *s_c], products)
    scale = -2.0 * tokens_all * features
    return finish(flags, upper, products, planes, teacher_norm.reshape(1, 1), scale)


def solution(mesh):
    sizes = (mesh.shape["tok"], mesh.shape["scol"], mesh.shape["tcol"])

    def body(student, teacher, teacher_norm):
        tokens_all = student.shape[0] * sizes[0]
        features = student.shape[1] * sizes[1]
        if sizes == (4, 4, 2) and tokens_all <= features:
            return token_form(student, teacher, teacher_norm)
        return feature_form(student, teacher, teacher_norm)

    return jax.shard_map(
        body,
        mesh=mesh,
        in_specs=(P("tok", "scol"), P("tok", "tcol"), P()),
        out_specs=P(("tok", "tcol"), "scol"),
        check_vma=False,
    )
```
